32 devices in a mesh: section: 4 (over x, core), band: 8 (over z, y).
Axes of the slice: x: 2, y: 2, z: 4, core: 2. Of those that a mesh axis runs over, the one named last changes fastest.
Arguments:
- images: float32 [8, 32, 192, 128], P(None, 'band'), may hold values from -6 to 6
- targets: float32 [8, 32, 192, 128], P(None, 'band'), may hold values from -12 to 12
- masks: int32 [8, 32, 192], P(None, 'band'), may hold values from 0 to 1, as said below
- conv_weights: float32 [4, 2, 3, 3, 128, 128], P('section'), may hold values from -0.1875 to 0.1875
- small_params: float32 [4, 6, 128], P('section'), may hold values from -3 to 3, as said below
- conv_first: float32 [4, 2, 3, 3, 128, 128], P('section'), may hold values from -0.00012207031 to 0.00012207031
- conv_second: float32 [4, 2, 3, 3, 128, 128], P('section'), may hold values from 8.4550866e-11 to 3.3820347e-10
- small_first: float32 [4, 6, 128], P('section'), may hold values from -0.0014648438 to 0.0014648438
- small_second: float32 [4, 6, 128], P('section'), may hold values from 8.455086e-09 to 3.3820346e-08
Outputs:
- new_conv: float32 [4, 2, 3, 3, 128, 128], P('section')
- new_conv_first: float32 [4, 2, 3, 3, 128, 128], P('section')
- new_conv_second: float32 [4, 2, 3, 3, 128, 128], P('section')
- new_small: float32 [4, 6, 128], P('section')
- new_small_first: float32 [4, 6, 128], P('section')
- new_small_second: float32 [4, 6, 128], P('section')
- loss_sum: float32 [], replicated
- valid_count: float32 [], replicated
- grad_norm: float32 [], replicated
The draws below stay inside these ranges and needn't reach their ends.
Inputs may be any that keep to these rules, and one draw needn't show every extreme that they name: `masks`: in every row of every image the ones form a prefix of the columns, and every row holds at least one. `small_params`: gains (rows 0 and 3) are positive.
All inputs are finite; a program needn't handle non-finite values.
Results may differ from the reference program's by a relative error of at most 0.0003.
Values sent between devices are 32-bit elements; how exact they have to be, the bound alone decides.
No kernel may reach another device: no remote copies, remote signals or barrier semaphores. Data moves between devices by JAX's collectives and lax.ppermute only.
A program may use at most 64 MiB of HBM per device.

```python
import math
import jax
import jax.numpy as jnp
from jax import lax

C = 128
GROUPS = 32
IMG_W = 192
MICRO = 8
STEP = 10
LAYERS = 4
HEIGHT = 32


def draw_masks(key, part):
    key = jax.random.fold_in(key, 11)
    first, second = jax.random.split(key)
    order = jax.random.permutation(first, MICRO)
    base = jnp.where(order < MICRO // 2, IMG_W, 2 * IMG_W // 3).astype(jnp.int32)
    rows = jnp.arange(HEIGHT, dtype=jnp.int32)
    cap = base[:, None] * (HEIGHT - 1 + 2 * rows[None, :]) // (3 * (HEIGHT - 1))
    lowest = (cap + 1) // 2
    valid = jax.random.randint(second, (MICRO, HEIGHT), lowest, cap + 1)
    cols = jnp.arange(IMG_W, dtype=jnp.int32)
    return (cols[None, None, :] < valid[:, :, None]).astype(jnp.int32)


def draw_small_params(key, part):
    key = jax.random.fold_in(key, 23)
    first, second = jax.random.split(key)
    noise = 0.3 * jax.random.normal(first, (LAYERS, 6, C), jnp.float32)
    gains = jax.random.uniform(second, (LAYERS, 6, C), jnp.float32, 0.6, 1.4)
    is_gain = (jnp.arange(6) % 3 == 0)[None, :, None]
    return jnp.clip(jnp.where(is_gain, gains, noise), -3.0, 3.0)


def shard_levels(own_key, shape, cuts, low, high):
    def one(axis_at, blocks):
        steps = jax.random.uniform(jax.random.fold_in(jax.random.fold_in(own_key, 6), axis_at), (blocks,), jnp.float32, low / len(cuts), high / len(cuts))
        return jnp.repeat(jnp.exp(steps), shape[axis_at] // blocks).reshape((-1,) + (1,) * (len(shape) - axis_at - 1))

    level = one(*cuts[0])
    for cut in cuts[1:]:
        level = level * one(*cut)
    return level


def centred(stream_key, dims, scale, limit, shards=(), held_as=jnp.bfloat16):
    level = shard_levels(stream_key, dims, shards, -0.22, 0.18) if shards else 1.0
    drawn = jax.random.normal(stream_key, dims, jnp.float32) * scale * level
    return jnp.minimum(jnp.maximum(drawn, -limit), limit).astype(held_as)


def setup_inputs(seed: int = 0) -> dict:
    keys = jax.random.split(jax.random.key(seed), 10)
    return {
        "images": centred(keys[0], (MICRO, HEIGHT, IMG_W, C), 1.0, 6.0, ((1, 8),), jnp.float32),
        "targets": centred(keys[1], (MICRO, HEIGHT, IMG_W, C), 2.0, 12.0, ((1, 8),), jnp.float32),
        "masks": draw_masks(jax.random.fold_in(keys[9], 71), 0),
        "conv_weights": centred(keys[3], (LAYERS, 2, 3, 3, C, C), (9 * C) ** -0.5, 0.1875, ((0, 4),), jnp.float32),
        "small_params": draw_small_params(jax.random.fold_in(keys[9], 71), 0),
        "conv_first": centred(keys[5], (LAYERS, 2, 3, 3, C, C), (0.01 * (LAYERS * (18 * C * C + 6 * C)) ** -0.5), 0.00012207031, ((0, 4),), jnp.float32),
        "conv_second": jnp.clip(jnp.exp(math.log(3.382034652332777e-10) - 1.3862944 * jax.random.uniform(keys[6], (LAYERS, 2, 3, 3, C, C), jnp.float32) ** shard_levels(keys[6], (LAYERS, 2, 3, 3, C, C), ((0, 4),), -0.2, 0.2)), 8.455086630831943e-11, 3.382034652332777e-10),
        "small_first": centred(keys[7], (LAYERS, 6, C), (0.1 * (LAYERS * (18 * C * C + 6 * C)) ** -0.5), 0.0014648438, ((0, 4),), jnp.float32),
        "small_second": jnp.clip(jnp.exp(math.log(3.382034563514935e-08) - 1.3862944 * jax.random.uniform(keys[8], (LAYERS, 6, C), jnp.float32) ** shard_levels(keys[8], (LAYERS, 6, C), ((0, 4),), -0.2, 0.2)), 8.455086408787338e-09, 3.382034563514935e-08),
    }


@jax.custom_vjp
def low(v):
    return lax.optimization_barrier(v.astype(jnp.bfloat16)).astype(jnp.float32)

@jax.custom_vjp
def low_back(v):
    return v

def low_keep(v):
    return (low(v), None)

def low_pass(kept, grad):
    return (grad,)

def back_keep(v):
    return (v, None)

def back_low(kept, grad):
    return (low(grad),)
low.defvjp(low_keep, low_pass)
low_back.defvjp(back_keep, back_low)

def group_norm(field, gain, shift):
    rows, width, chans = field.shape
    per = chans // GROUPS
    grouped = field.reshape(rows, width, GROUPS, per)
    count = rows * width * per
    mean = lax.optimization_barrier(jnp.sum(grouped, (0, 1, 3))) / count
    var = lax.optimization_barrier(jnp.sum(grouped * grouped, (0, 1, 3))) / count - mean * mean
    inv = lax.rsqrt(var + 1e-05)
    normed = ((grouped - mean[:, None]) * inv[:, None]).reshape(field.shape)
    return normed * gain + shift

def convolve(field, kernel, bias):
    out = lax.conv_general_dilated(field[None], kernel, (1, 1), ((1, 1), (1, 1)), dimension_numbers=('NHWC', 'HWIO', 'NHWC'), precision=lax.Precision.HIGHEST)[0]
    return out + bias

def block(field, kernels, small):
    mid = convolve(jax.nn.silu(group_norm(field, small[0], small[1])), kernels[0], small[2])
    return field + convolve(jax.nn.silu(group_norm(mid, small[3], small[4])), kernels[1], small[5])

def micro_loss(conv_weights, small_params, image, target, mask):

    def layer(state, params):
        return (jax.checkpoint(block)(state, params[0], params[1]), None)
    final, _ = lax.scan(layer, image, (conv_weights, small_params))
    diff = final - target
    weight = mask.astype(jnp.float32)[:, :, None]
    return jnp.sum(weight * (jnp.sqrt(diff * diff + 1.0) - 1.0))

def reference(images, targets, masks, conv_weights, small_params, conv_first, conv_second, small_first, small_second):
    valid_count = jnp.sum(masks.astype(jnp.float32))

    def one_micro(carry, inputs):
        loss_acc, conv_acc, small_acc = carry
        image, target, mask = inputs
        value, pullback = jax.vjp(lambda a, b: micro_loss(a, b, image, target, mask), conv_weights, small_params)
        conv_grad, small_grad = pullback(jnp.float32(1.0) / valid_count)
        return ((loss_acc + value, conv_acc + conv_grad, small_acc + small_grad), None)
    start = (jnp.float32(0.0), jnp.zeros_like(conv_weights), jnp.zeros_like(small_params))
    (loss_sum, conv_grad, small_grad), _ = lax.scan(one_micro, start, (images, targets, masks))
    grad_norm = jnp.sqrt(jnp.sum(conv_grad * conv_grad) + jnp.sum(small_grad * small_grad))
    clip = 0.01 / jnp.maximum(grad_norm, 0.01)

    def adam(weight, first, second, grad, rate):
        grad = grad * clip
        first = 0.5 * first + 0.5 * grad
        second = 0.5 * second + 0.5 * grad * grad
        fix_one = 1.0 - 0.5 ** STEP
        fix_two = 1.0 - 0.5 ** STEP
        step = first / fix_one / (jnp.sqrt(second / fix_two) + 1e-08) + 0.01 * weight
        return (weight - rate * step, first, second)
    new_conv, new_conv_first, new_conv_second = adam(conv_weights, conv_first, conv_second, conv_grad, 0.02)
    new_small, new_small_first, new_small_second = adam(small_params, small_first, small_second, small_grad, 0.2)
    return (new_conv, new_conv_first, new_conv_second, new_small, new_small_first, new_small_second, loss_sum, valid_count, grad_norm)
```

```python
import functools

import jax
import jax.numpy as jnp
from jax import lax
from jax.experimental import pallas as pl
from jax.experimental.pallas import tpu as pltpu
from jax.sharding import PartitionSpec as P

GROUPS = 32
STEP = 10
PAIR = 2

clip_level = 0.01
rate_conv = 0.02
rate_small = 0.2
adam_eps = 1e-08
decay_rate = 0.01

BF = jnp.bfloat16
F32 = jnp.float32
VM = pl.BlockSpec(memory_space=pltpu.VMEM)
SM = pl.BlockSpec(memory_space=pltpu.SMEM)
HB = pl.BlockSpec(memory_space=pltpu.HBM)


def split(x):
    hi = x.astype(BF)
    return hi, (x - hi.astype(F32)).astype(BF)


def group_sum(row, per):
    lane = lax.broadcasted_iota(jnp.int32, row.shape, 1)
    width = row.shape[1]
    step = 1
    while step < per:
        other = jnp.where(
            (lane // step) % 2 == 0, pltpu.roll(row, width - step, 1), pltpu.roll(row, step, 1)
        )
        row = row + other
        step *= 2
    return row


def sigmoid(u):
    return 0.5 * jnp.tanh(0.5 * u) + 0.5


def put_columns(hi_ref, lo_ref, at, field):
    n, _, half, c = field.shape
    even, odd = field[:, 0], field[:, 1]
    k = lax.broadcasted_iota(jnp.int32, (n, half, c), 1)
    down = jnp.where(k == 0, 0.0, pltpu.roll(odd, 1, 1))
    up = jnp.where(k == half - 1, 0.0, pltpu.roll(even, half - 1, 1))
    for q, part in enumerate((down, even, odd, up)):
        hi, lo = split(part)
        hi_ref[pl.ds(at, n), :, q * c : (q + 1) * c] = hi
        lo_ref[pl.ds(at, n), :, q * c : (q + 1) * c] = lo


def put_edges(hi_ref, lo_ref, side, cols, edge):
    put_columns(hi_ref, lo_ref, 0, jnp.where(side == 1, edge, 0.0))
    put_columns(hi_ref, lo_ref, cols + 1, jnp.where(side == 0, edge, 0.0))


def taps(ref, at, n):
    _, half, width = ref.shape
    return jnp.concatenate(
        [ref[pl.ds(at + t, n)].reshape(n * half, width) for t in range(3)], axis=1
    )


def pair_rows(one, two):
    return jnp.concatenate(
        [one.sum(0, keepdims=True), two.sum(0, keepdims=True), jnp.zeros((6, one.shape[1]), F32)], 0
    )


def chunk_of(cols, most):
    return max(n for n in range(1, most + 1) if cols % n == 0)


NEAR = 2 << 20


def is_near(x):
    return x.size * 4 <= NEAR


def room_for(field, fields):
    fields = 1 if is_near(field) else fields
    return pltpu.CompilerParams(vmem_limit_bytes=fields * field.size * 4 + (10 << 20))


def result(shape):
    near = pltpu.VMEM(shape, F32)
    return near if is_near(jax.ShapeDtypeStruct(shape, F32)) else jax.ShapeDtypeStruct(shape, F32)


def held(args):
    return [
        pltpu.with_memory_space_constraint(x, pltpu.VMEM) if x.ndim == 4 and is_near(x) else x
        for x in args
    ]


def far(args):
    return [pltpu.with_memory_space_constraint(x, pltpu.HBM) for x in args]


def fetch(pick, which, sources, into, sem):
    for k, source in enumerate(sources):

        @pl.when(pick == k)
        def _(source=source):
            pltpu.make_async_copy(source.at[which], into, sem).start()


def fetched(which, sources, into, sem):
    pltpu.make_async_copy(sources[0].at[which], into, sem).wait()


def pack_forward(w_ref, hi_ref, lo_ref):
    c = w_ref.shape[-1]
    zero = jnp.zeros((c, c), BF)
    for t in range(3):
        for q in range(4):
            at = (t * 4 + q) * c
            for p in range(2):
                hi, lo = split(w_ref[q - p, t]) if 0 <= q - p < 3 else (zero, zero)
                hi_ref[at : at + c, p * c : (p + 1) * c] = hi
                lo_ref[at : at + c, p * c : (p + 1) * c] = lo


def pack_backward(w_ref, hi_ref, lo_ref):
    c = w_ref.shape[-1]
    zero = jnp.zeros((c, c), BF)
    for t in range(3):
        for q in range(4):
            at = (t * 4 + q) * c
            for p in range(2):
                hi, lo = split(w_ref[2 - (q - p), 2 - t]) if 0 <= q - p < 3 else (zero, zero)
                hi_ref[p * c : (p + 1) * c, at : at + c] = hi
                lo_ref[p * c : (p + 1) * c, at : at + c] = lo


RUN = 32


def in_turns(unrolled, cols, fill, ready, conv, carry):
    if not unrolled:
        n = chunk_of(cols, 4)
        carry = lax.fori_loop(0, cols // n, lambda j, c: fill(j * n, n, c), carry)
        ready()
        return lax.fori_loop(0, cols // n, lambda j, c: conv(j * n, n, c), carry)
    n = chunk_of(cols, RUN)
    done = min(cols, n + 2)
    carry = fill(0, done, carry)
    ready()
    for at in range(0, cols, n):
        carry = conv(at, n, carry)
        more = min(n, cols - done)
        if more > 0:
            carry = fill(done, more, carry)
            done += more
    return carry


def forward_kernel(sources, following, with_res, *refs):
    refs = list(refs)
    take = lambda n: [refs.pop(0) for _ in range(n)]
    info_ref, next_ref, w_ref, v_ref, in_ref, own_ref, small_ref = take(7)
    res_ref = take(1)[0] if with_res else None
    source_refs = take(sources)
    out_ref, msg_ref, norm_ref, after_ref, hi_ref, lo_ref, whi_ref, wlo_ref, sem = refs
    cols, _, half, c = v_ref.shape
    rows = 2 * half
    side = info_ref[0]
    fetch(next_ref[1], following, source_refs, after_ref, sem)
    per = c // GROUPS
    count = float(PAIR * cols * rows * per)
    sums = group_sum(own_ref[rows : rows + 8, :] + in_ref[rows : rows + 8, :], per) / count
    mean = sums[0:1]
    inv = lax.rsqrt(sums[1:2] - mean * mean + 1e-05)
    norm_ref[0:1, :] = mean
    norm_ref[1:2, :] = inv
    norm_ref[2:8, :] = jnp.zeros((6, c), F32)
    gain = inv * small_ref[0:1, :]
    shift = small_ref[1:2, :]
    bias = small_ref[2:3, :]

    def act(x):
        u = (x - mean) * gain + shift
        return u * sigmoid(u)

    put_edges(hi_ref, lo_ref, side, cols, act(in_ref[0:rows, :].reshape(1, 2, half, c)))

    def ready():
        pack_forward(w_ref, whi_ref, wlo_ref)

    def fill(at, n, carry):
        put_columns(hi_ref, lo_ref, 1 + at, act(v_ref[pl.ds(at, n)]))
        return carry

    def conv(at, n, carry):
        one, two = carry
        hi = taps(hi_ref, at, n)
        acc = jnp.dot(hi, whi_ref[...], preferred_element_type=F32)
        acc += jnp.dot(hi, wlo_ref[...], preferred_element_type=F32)
        acc += jnp.dot(taps(lo_ref, at, n), whi_ref[...], preferred_element_type=F32)
        for p in range(2):
            o = (acc[:, p * c : (p + 1) * c] + bias).reshape(n, half, c)
            if with_res:
                o = o + res_ref[pl.ds(at, n), p]
            out_ref[pl.ds(at, n), p] = o
            f = o.reshape(-1, 8, c)
            one = one + f.sum(0)
            two = two + (f * f).sum(0)
        return one, two

    zero = jnp.zeros((8, c), F32)
    one, two = in_turns(is_near(v_ref), cols, fill, ready, conv, (zero, zero))
    last = jnp.where(side == 0, cols - 1, 0)
    msg_ref[0:rows, :] = out_ref[pl.ds(last, 1)].reshape(rows, c)
    msg_ref[rows : rows + 8, :] = pair_rows(one, two)
    fetched(following, source_refs, after_ref, sem)


def conv_scratch(cols, half, c, packed):
    return (
        [pltpu.VMEM((cols + 2, half, 4 * c), BF)] * 2
        + [pltpu.VMEM(packed, BF)] * 2
        + [pltpu.SemaphoreType.DMA(())]
    )


def conv_forward(info, weights, v, msg_in, msg_own, small, res=None):
    cols, _, half, c = v.shape
    rows = 2 * half
    w, sources, (info_next, following) = weights
    args = [info, info_next, w, v, msg_in, msg_own, small] + ([] if res is None else [res])
    pixels = cols * rows
    return pl.pallas_call(
        functools.partial(forward_kernel, len(sources), following, res is not None),
        out_shape=[result(v.shape), result((rows + 8, c)), result((8, c)), result(w.shape)],
        in_specs=[SM, SM] + [VM] * (len(args) - 2) + [HB] * len(sources),
        out_specs=[VM] * 4,
        scratch_shapes=conv_scratch(cols, half, c, (12 * c, 2 * c)),
        compiler_params=room_for(v, 6),
        cost_estimate=pl.CostEstimate(
            flops=pixels * 72 * c * c, bytes_accessed=pixels * c * 8, transcendentals=pixels * c
        ),
    )(*held(args), *far(sources))


def enter_norm(own_ref, in_ref, norm_ref, small_ref, cols, rows):
    c = own_ref.shape[-1]
    per = c // GROUPS
    count = float(PAIR * cols * rows * per)
    gain = small_ref[0:1, :]
    mean = norm_ref[0:1, :]
    inv = norm_ref[1:2, :]
    sums = own_ref[rows : rows + 8, :] + in_ref[rows : rows + 8, :]
    means = group_sum(sums * gain, per) / count
    first, second = means[0:1], means[1:2]

    def enter(t, v):
        return inv * (t * gain - first - (v - mean) * inv * second)

    return enter


def enter_kernel(t_ref, in_ref, own_ref, v_ref, edge_ref, norm_ref, small_ref, g_ref, ge_ref, bias_ref):
    cols, _, half, c = t_ref.shape
    rows = 2 * half
    enter = enter_norm(own_ref, in_ref, norm_ref, small_ref, cols, rows)
    edge = enter(in_ref[0:rows, :], edge_ref[0:rows, :])
    ge_ref[0:rows, :] = edge
    ge_ref[rows : rows + 8, :] = jnp.zeros((8, c), F32)
    n = chunk_of(cols, 8)

    def fill(j, total):
        at = pl.ds(j * n, n)
        g = enter(t_ref[at], v_ref[at])
        g_ref[at] = g
        return total + g.reshape(-1, 8, c).sum(0)

    total = lax.fori_loop(0, cols // n, fill, jnp.zeros((8, c), F32))
    bias_ref[...] = jnp.broadcast_to(total.sum(0, keepdims=True), (8, c))


def norm_enter(t, msg_in, norm):
    cols, _, half, c = t.shape
    return pl.pallas_call(
        enter_kernel,
        out_shape=[
            result(t.shape),
            result((2 * half + 8, c)),
            result((8, c)),
        ],
        in_specs=[VM] * 7,
        out_specs=[VM] * 3,
        compiler_params=room_for(t, 4),
    )(*held([t, msg_in, *norm]))


def backward_kernel(sources, following, with_norm, with_res, *refs):
    refs = list(refs)
    take = lambda n: [refs.pop(0) for _ in range(n)]
    info_ref, next_ref, w_ref, t_ref, in_ref = take(5)
    if with_norm:
        own_ref, vp_ref, vpe_ref, normp_ref, smallp_ref = take(5)
    if with_res:
        res_ref, rese_ref = take(2)
    ve_ref, norme_ref, smalle_ref = take(3)
    source_refs = take(sources)
    if with_norm:
        g_ref, ge_ref = take(2)
    out_ref, msg_ref, bias_ref, after_ref, hi_ref, lo_ref, bhi_ref, blo_ref, sem = refs
    cols, _, half, c = t_ref.shape
    rows = 2 * half
    side = info_ref[0]
    fetch(next_ref[1], following, source_refs, after_ref, sem)
    edge = in_ref[0:rows, :]
    if with_norm:
        enter = enter_norm(own_ref, in_ref, normp_ref, smallp_ref, cols, rows)
        edge = enter(edge, vpe_ref[0:rows, :])
        if with_res:
            edge = edge + rese_ref[0:rows, :]
        ge_ref[0:rows, :] = edge
        ge_ref[rows : rows + 8, :] = jnp.zeros((8, c), F32)
    put_edges(hi_ref, lo_ref, side, cols, edge.reshape(1, 2, half, c))
    zero = jnp.zeros((8, c), F32)

    def ready():
        pack_backward(w_ref, bhi_ref, blo_ref)

    def fill(at, n, carry):
        one, two, total = carry
        run = pl.ds(at, n)
        g = t_ref[run]
        if with_norm:
            g = enter(g, vp_ref[run])
            if with_res:
                g = g + res_ref[run]
            g_ref[run] = g
        put_columns(hi_ref, lo_ref, 1 + at, g)
        return one, two, total + g.reshape(-1, 8, c).sum(0)

    gain_e, shift_e = smalle_ref[0:1, :], smalle_ref[1:2, :]
    mean_e, inv_e = norme_ref[0:1, :], norme_ref[1:2, :]

    def dot(a, b):
        return lax.dot_general(a, b, (((1,), (1,)), ((), ())), preferred_element_type=F32)

    def conv(at, n, carry):
        one, two, total = carry
        hi = taps(hi_ref, at, n)
        acc = dot(hi, bhi_ref[...])
        acc += dot(hi, blo_ref[...])
        acc += dot(taps(lo_ref, at, n), bhi_ref[...])
        for p in range(2):
            q = acc[:, p * c : (p + 1) * c].reshape(n, half, c)
            normed = (ve_ref[pl.ds(at, n), p] - mean_e) * inv_e
            u = normed * gain_e + shift_e
            s = sigmoid(u)
            t = q * (s * (1.0 + u * (1.0 - s)))
            out_ref[pl.ds(at, n), p] = t
            one = one + t.reshape(-1, 8, c).sum(0)
            two = two + (t * normed).reshape(-1, 8, c).sum(0)
        return one, two, total

    one, two, total = in_turns(is_near(t_ref), cols, fill, ready, conv, (zero, zero, zero))
    bias_ref[...] = jnp.broadcast_to(total.sum(0, keepdims=True), (8, c))
    last = jnp.where(side == 0, cols - 1, 0)
    msg_ref[0:rows, :] = out_ref[pl.ds(last, 1)].reshape(rows, c)
    msg_ref[rows : rows + 8, :] = pair_rows(one, two)
    fetched(following, source_refs, after_ref, sem)


def conv_backward(info, weights, t, msg_in, v_e, norm_e, small_e, norm=None, res=None):
    cols, _, half, c = t.shape
    rows = 2 * half
    w, sources, (info_next, following) = weights
    args = [info, info_next, w, t, msg_in] + list(norm or ()) + list(res or ())
    args += [v_e, norm_e, small_e]
    field, msg = result(t.shape), result((rows + 8, c))
    outs = ([field, msg] if norm else []) + [field, msg, result((8, c)), result(w.shape)]
    pixels = cols * rows
    places = {}
    if norm and not is_near(t):
        places = {3: 2, 10: 0} if res else {3: 2}
    got = pl.pallas_call(
        functools.partial(backward_kernel, len(sources), following, norm is not None, res is not None),
        out_shape=outs,
        input_output_aliases=places,
        in_specs=[SM, SM] + [VM] * (len(args) - 2) + [HB] * len(sources),
        out_specs=[VM] * len(outs),
        scratch_shapes=conv_scratch(cols, half, c, (2 * c, 12 * c)),
        compiler_params=room_for(t, 8),
        cost_estimate=pl.CostEstimate(
            flops=pixels * 72 * c * c, bytes_accessed=pixels * c * 16, transcendentals=pixels * c
        ),
    )(*held(args), *far(sources))
    return got if norm else [t, msg_in] + list(got)


def kernel_grad_kernel(with_prev, *refs):
    refs = list(refs)
    info_ref, v_ref, edge_ref, norm_ref, small_ref, g_ref = refs[:6]
    prev_ref = refs[6] if with_prev else None
    out_ref, hi_ref, lo_ref, ghi_ref, glo_ref = refs[6 + with_prev :]
    cols, _, half, c = v_ref.shape
    rows = 2 * half
    mine = info_ref[2] == 1

    @pl.when(jnp.logical_not(mine))
    def _():
        out_ref[...] = prev_ref[...] if with_prev else jnp.zeros_like(out_ref)

    @pl.when(mine)
    def _():
        mean = norm_ref[0:1, :]
        gain = norm_ref[1:2, :] * small_ref[0:1, :]
        shift = small_ref[1:2, :]

        def act(x):
            u = (x - mean) * gain + shift
            return u * sigmoid(u)

        edge = act(edge_ref[0:rows, :].reshape(1, 2, half, c))
        put_edges(hi_ref, lo_ref, info_ref[0], cols, edge)
        fill_n = chunk_of(cols, 8)

        def fill(j, _):
            at = j * fill_n
            put_columns(hi_ref, lo_ref, 1 + at, act(v_ref[pl.ds(at, fill_n)]))
            for p in range(2):
                hi, lo = split(g_ref[pl.ds(at, fill_n), p])
                ghi_ref[pl.ds(at, fill_n), :, p * c : (p + 1) * c] = hi
                glo_ref[pl.ds(at, fill_n), :, p * c : (p + 1) * c] = lo
            return 0

        lax.fori_loop(0, cols // fill_n, fill, 0)

        def dot(a, b):
            return lax.dot_general(a, b, (((0,), (0,)), ((), ())), preferred_element_type=F32)

        def products(at, n, add):
            ghi = ghi_ref[pl.ds(at, n)].reshape(n * half, 2 * c)
            glo = glo_ref[pl.ds(at, n)].reshape(n * half, 2 * c)
            for t in range(3):
                hi = hi_ref[pl.ds(at + t, n)].reshape(n * half, 4 * c)
                lo = lo_ref[pl.ds(at + t, n)].reshape(n * half, 4 * c)
                acc = dot(hi, ghi) + dot(hi, glo) + dot(lo, ghi)
                for a in range(3):
                    to = slice((a * 3 + t) * c, (a * 3 + t + 1) * c)
                    new = acc[a * c : (a + 1) * c, :c] + acc[(a + 1) * c : (a + 2) * c, c:]
                    out_ref[to, :] = out_ref[to, :] + new if add else new

        if is_near(v_ref):
            products(0, cols, False)
        else:
            n = chunk_of(cols, 8)
            out_ref[...] = jnp.zeros_like(out_ref)
            lax.fori_loop(0, cols // n, lambda j, _: (products(j * n, n, True), 0)[1], 0)


def kernel_grad(info, v, edge, norm, small, g, prev=None):
    cols, _, half, c = v.shape
    pixels = cols * half * 2
    args = [info, v, edge, norm, small, g] + ([] if prev is None else [prev])
    return pl.pallas_call(
        functools.partial(kernel_grad_kernel, prev is not None),
        out_shape=result((9 * c, c)),
        in_specs=[SM] + [VM] * (len(args) - 1),
        out_specs=VM,
        scratch_shapes=[pltpu.VMEM((cols + 2, half, 4 * c), BF)] * 2
        + [pltpu.VMEM((cols, half, 2 * c), BF)] * 2,
        compiler_params=room_for(v, 6),
        cost_estimate=pl.CostEstimate(
            flops=pixels * 72 * c * c, bytes_accessed=pixels * c * 8, transcendentals=pixels * c
        ),
    )(*held(args))


def from_rows(ref, at, n, p):
    half = ref.shape[0] // 2
    return jnp.swapaxes(ref[pl.ds(p, half, stride=2), pl.ds(at, n), :], 0, 1)


def arrive_kernel(sources, info_ref, raw_ref, *refs):
    source_refs, (out_ref, msg_ref, after_ref, sem) = refs[:sources], refs[sources:]
    fetch(info_ref[1], 0, source_refs, after_ref, sem)
    rows, cols, c = raw_ref.shape
    one = two = jnp.zeros((8, c), F32)
    run = chunk_of(cols, RUN)
    for at in range(0, cols, run):
        for p in range(2):
            x = from_rows(raw_ref, at, run, p)
            out_ref[at : at + run, p] = x
            f = x.reshape(-1, 8, c)
            one = one + f.sum(0)
            two = two + (f * f).sum(0)
    last = jnp.where(info_ref[0] == 0, cols - 1, 0)
    msg_ref[0:rows, :] = out_ref[pl.ds(last, 1)].reshape(rows, c)
    msg_ref[rows : rows + 8, :] = pair_rows(one, two)
    fetched(0, source_refs, after_ref, sem)


def arrived(info, raw, sources):
    rows, cols, c = raw.shape
    return pl.pallas_call(
        functools.partial(arrive_kernel, len(sources)),
        out_shape=[result((cols, 2, rows // 2, c)), result((rows + 8, c)), result((3, 3, c, c))],
        in_specs=[SM, VM] + [HB] * len(sources),
        out_specs=[VM] * 3,
        scratch_shapes=[pltpu.SemaphoreType.DMA(())],
        compiler_params=room_for(raw, 4),
    )(info, raw, *far(sources))


def loss_kernel(repeats, info_ref, final_ref, raw_ref, g_ref, msg_ref, count_ref, valid_ref):
    cols, _, half, c = final_ref.shape
    rows = 2 * half
    side = info_ref[0]
    count = jnp.zeros((1, c), F32)
    for p in range(2):
        extra = from_rows(raw_ref, cols, 8, p)
        valid_ref[p] = extra[0]
        count = count + extra[1].sum(0, keepdims=True)
    count_ref[...] = jnp.broadcast_to(count, (8, c))
    scale = 1.0 / (count * repeats)
    n = chunk_of(cols, 8)

    def step(j, total):
        at = pl.multiple_of(j * n, n)
        column = (lax.broadcasted_iota(jnp.int32, (n, half, c), 0) + (side * cols + at)).astype(F32)
        for p in range(2):
            diff = final_ref[pl.ds(at, n), p] - from_rows(raw_ref, at, n, p)
            square = diff * diff + 1.0
            valid = column < valid_ref[p][None]
            g_ref[pl.ds(at, n), p] = jnp.where(valid, diff * lax.rsqrt(square) * scale, 0.0)
            part = jnp.where(valid, jnp.sqrt(square) - 1.0, 0.0)
            total = total + part.reshape(-1, 8, c).sum(0)
        return total

    total = lax.fori_loop(0, cols // n, step, jnp.zeros((8, c), F32))
    last = jnp.where(side == 0, cols - 1, 0)
    msg_ref[0:rows, :] = g_ref[pl.ds(last, 1)].reshape(rows, c)
    msg_ref[rows : rows + 8, :] = total


def loss_and_gradient(info, final, raw, repeats):
    cols, _, half, c = final.shape
    return pl.pallas_call(
        functools.partial(loss_kernel, repeats),
        out_shape=[result(final.shape), result((2 * half + 8, c)), result((8, c))],
        in_specs=[SM] + [VM] * 2,
        out_specs=[VM] * 3,
        scratch_shapes=[pltpu.VMEM((2, half, c), F32)],
        compiler_params=room_for(final, 5),
    )(info, *held([final]), raw)


def adam_kernel(
    info_ref, clip_ref, w_ref, first_ref, second_ref, odd_ref, even_ref, got_ref, w_out, first_out, second_out
):
    mine = info_ref[0] == 0
    clip = clip_ref[0]
    fix = 1.0 - 0.5**STEP
    n = 9 * w_ref.shape[-1] // 8

    def step(j, _):
        at = pl.ds(pl.multiple_of(j * n, 8), n)
        for which in range(2):
            if which == 0:
                grad = jnp.where(mine, even_ref[at, :], got_ref[at, :])
            else:
                grad = jnp.where(mine, got_ref[at, :], odd_ref[at, :])
            grad = grad * clip
            w = w_ref[which, at, :]
            first = 0.5 * first_ref[which, at, :] + 0.5 * grad
            second = 0.5 * second_ref[which, at, :] + 0.5 * grad * grad
            step = first / fix / (jnp.sqrt(second / fix) + adam_eps) + decay_rate * w
            w_out[which, at, :] = w - rate_conv * step
            first_out[which, at, :] = first
            second_out[which, at, :] = second
        return 0

    lax.fori_loop(0, 8, step, 0)


def adam_blocks(info, clip, weight, first, second, odd, even, got):
    out = jax.ShapeDtypeStruct(weight.shape, F32)
    return pl.pallas_call(
        adam_kernel,
        out_shape=[out] * 3,
        in_specs=[SM, SM] + [VM] * 6,
        out_specs=[VM] * 3,
        compiler_params=pltpu.CompilerParams(vmem_limit_bytes=12 * weight.size * 4),
    )(info, clip, weight, first, second, odd, even, got)


def partner(x):
    return lax.ppermute(x, "section", [(i, i ^ 1) for i in range(lax.axis_size("section"))])


def to_image(bands, repeats):
    bands = jnp.repeat(bands, repeats, 0) if repeats > 1 else bands
    got = lax.all_to_all(bands, "band", 0, 0, tiled=True)
    return got.reshape(-1, *got.shape[2:])


def crossed(x, by):
    return lax.ppermute(x, "band", [(i, i ^ by) for i in range(lax.axis_size("band"))])


def band_bits():
    return [1 << k for k in range(lax.axis_size("band").bit_length() - 1)]


def halved(block, by):
    n = block.shape[0] // 2
    upper = (lax.axis_index("band") // by) % 2 == 1
    low, high = block[:n], block[n:]
    return jnp.where(upper, high, low) + crossed(jnp.where(upper, low, high), by)


def doubled(block, by):
    other = crossed(block, by)
    upper = (lax.axis_index("band") // by) % 2 == 1
    return jnp.concatenate([jnp.where(upper, other, block), jnp.where(upper, block, other)], 0)


def share_sum(block):
    bands = lax.axis_size("band")
    parts = block.reshape(bands, -1, block.shape[-1])
    return lax.all_to_all(parts, "band", 0, 0, tiled=True).sum(0)


def gather_shares(share):
    bands = lax.axis_size("band")
    return lax.all_to_all(jnp.broadcast_to(share, (bands, *share.shape)), "band", 0, 0, tiled=True)


def adam_rows(weight, first, second, grad, rates):
    first = 0.5 * first + 0.5 * grad
    second = 0.5 * second + 0.5 * grad * grad
    fix_one = 1.0 - 0.5**STEP
    fix_two = 1.0 - 0.5**STEP
    step = first / fix_one / (jnp.sqrt(second / fix_two) + adam_eps) + decay_rate * weight
    return (weight - rates * step, first, second)


def local(
    images,
    targets,
    masks,
    conv_weights,
    small_params,
    conv_first,
    conv_second,
    small_first,
    small_second,
):
    sections = lax.axis_size("section")
    bands = lax.axis_size("band")
    here = lax.axis_index("section")
    core = here % PAIR
    chip = here // PAIR
    chips = sections // PAIR
    layers = sections
    micro, part, width, c = images.shape
    repeats = bands // micro
    cols = width // PAIR
    rows = part * bands
    half = rows // 2

    image = to_image(lax.dynamic_slice_in_dim(images, core * cols, cols, 2), repeats)
    lengths = jnp.sum(masks.astype(F32), 2)
    counts = jnp.where(jnp.arange(part)[None, :] == 0, jnp.sum(lengths), 0.0)
    extra = jnp.stack([lengths, jnp.broadcast_to(counts, lengths.shape)] + [jnp.zeros_like(lengths)] * 6, 2)
    extra = jnp.broadcast_to(extra[..., None], (micro, part, 8, c))
    target = jnp.concatenate([lax.dynamic_slice_in_dim(targets, core * cols, cols, 2), extra], 2)
    image, target = lax.optimization_barrier((image, target))
    target = to_image(target, repeats)

    own = (conv_weights[0], jnp.pad(small_params[0], ((0, 2), (0, 0))))
    sources, smalls = [], []
    for k in range(chips):
        shift = [((i + PAIR * k) % sections, i) for i in range(sections)]
        theirs = own if k == 0 else tuple(lax.ppermute(x, "section", shift) for x in own)
        others = tuple(partner(x) for x in theirs)
        sources += [theirs[0], others[0]]
        smalls += [theirs[1], others[1]]
    smalls = jnp.stack(smalls)

    def pick_of(layer):
        return PAIR * ((layer // PAIR - chip) % chips) + (layer % PAIR != core).astype(jnp.int32)

    def info_of(layer):
        mine = (chip == layer // PAIR).astype(jnp.int32)
        return jnp.stack([core, pick_of(layer), mine]).astype(jnp.int32)

    def norms_of(layer):
        both = lax.dynamic_index_in_dim(smalls, pick_of(layer), 0, False)
        return jnp.pad(both[0:3], ((0, 5), (0, 0))), jnp.pad(both[3:6], ((0, 5), (0, 0)))

    infos = [info_of(l) for l in range(layers)]
    norms = [norms_of(l) for l in range(layers)]
    image, infos, norms = lax.optimization_barrier((image, infos, norms))
    again_first = not is_near(jax.ShapeDtypeStruct((cols, rows, c), F32))
    order = [(l, k) for l in range(layers) for k in range(2)]
    for l in reversed(range(layers)):
        order += [(l, 0)] * again_first + [(l, 1), (l, 0)]
    order = [(infos[l], k) for l, k in order[1:]] + [(infos[0], 0)]

    def with_next(w):
        return w, sources, order.pop(0)

    field, message, w = arrived(infos[0], image, sources)
    stack = []
    for l in range(layers):
        got = partner(message)
        mid, sent, norm, w = conv_forward(infos[l], with_next(w), field, got, message, norms[l][0])
        again = partner(sent)
        one, first_in = (field, got, norm), (field, got, message, norms[l][0])
        field, message, norm, w = conv_forward(
            infos[l], with_next(w), mid, again, sent, norms[l][1], field
        )
        stack.append((one, (None if again_first else mid, again, norm), first_in))

    def second_back(l, w, t, got, enter, res, prev):
        _, (v2, e2, n2), first_in = stack[l]
        if again_first:
            t, first_in = lax.optimization_barrier((t, first_in))
            v2, _, _, w = conv_forward(infos[l], with_next(w), *first_in)
        grad, grad_edge, t, sent, bias, w = conv_backward(
            infos[l], with_next(w), t, got, v2, n2, norms[l][1], norm=enter, res=res
        )
        got = partner(sent)
        k2 = kernel_grad(infos[l], v2, e2, n2, norms[l][1], grad, prev)
        return k2, bias, w, t, got, (sent, v2, e2, n2, norms[l][1]), (grad, grad_edge)

    def small_grad_of(l, one, bias1, two, bias2):
        one, two = one[rows : rows + 2], two[rows : rows + 2]
        parts = [one[1:2], one[0:1], bias1[0:1], two[1:2], two[0:1], bias2[0:1]]
        return jnp.where(infos[l][2] == 1, jnp.concatenate(parts, 0), 0.0)

    def across_cores(k1, k2):
        return jnp.where(core == 0, k1, k2) + partner(jnp.where(core == 0, k2, k1))

    grad, message, count = loss_and_gradient(infos[0], field, target, repeats)
    valid_count = count[0, 0]
    got = partner(message)
    loss_rows = message

    t, enter, res = grad, None, None
    slots = [[None, None] for _ in range(PAIR)]
    pieces = {}
    for l in reversed(range(1, layers)):
        slot = slots[l % PAIR]
        k2, bias2, w, t, got, enter, res = second_back(l, w, t, got, enter, res, slot[1])
        sent = enter[0]
        v1, e1, n1 = stack[l][0]
        mid, _, t, message, bias1, w = conv_backward(
            infos[l], with_next(w), t, got, v1, n1, norms[l][0], norm=enter
        )
        got = partner(message)
        k1 = kernel_grad(infos[l], v1, e1, n1, norms[l][0], mid, slot[0])
        enter = (message, v1, e1, n1, norms[l][0])
        slot[:] = [k1, k2]
        pieces[l] = (message, bias1, sent, bias2)

    odd = across_cores(*slots[1])
    k2, bias2, w, t, got, enter, res = second_back(0, w, t, got, enter, res, slots[0][1])
    for by in band_bits():
        odd = halved(odd, by)
    sent = enter[0]
    v1, e1, n1 = stack[0][0]
    mid, mid_edge, bias1 = norm_enter(t, got, enter)
    k1 = kernel_grad(infos[0], v1, e1, n1, norms[0][0], mid, slots[0][0])
    _, _, _, message, _, _ = conv_backward(
        infos[0], with_next(w), mid, mid_edge, v1, n1, norms[0][0]
    )
    pieces[0] = (message, bias1, sent, bias2)
    k1, pieces, loss_rows = lax.optimization_barrier((k1, pieces, loss_rows))
    small_even, small_odd = [
        sum(small_grad_of(l, *pieces[l]) for l in range(p, layers, PAIR)) for p in range(PAIR)
    ]
    loss_row = jnp.sum(loss_rows[rows : rows + 8], 0, keepdims=True)
    even = share_sum(across_cores(k1, k2))
    squares = jnp.sum(odd * odd, 0, keepdims=True) + jnp.sum(even * even, 0, keepdims=True)
    for by in reversed(band_bits()):
        odd = doubled(odd, by)
    rest = jnp.concatenate(
        [even, small_even, small_odd, loss_row, squares, jnp.zeros((2, c), F32)], 0
    )
    rest = gather_shares(rest)
    n = even.shape[0]
    even = rest[:, :n].reshape(-1, c)
    table = jnp.sum(rest[:, n:], 0)
    first_core = core == 0
    got = partner(jnp.where(first_core, odd, even))
    table = table + partner(table)
    loss_sum = jnp.sum(table[12]) / repeats
    norm_sq = jnp.sum(table[13]) + jnp.sum(table[:12] * table[:12])
    by = PAIR
    while by < sections:
        norm_sq = norm_sq + lax.ppermute(norm_sq, "section", [(i, i ^ by) for i in range(sections)])
        by *= 2
    grad_norm = jnp.sqrt(norm_sq)
    clip = clip_level / jnp.maximum(grad_norm, clip_level)

    flat = lambda x: x.reshape(2, 9 * c, c)
    new = adam_blocks(
        infos[0], clip.reshape(1), flat(conv_weights), flat(conv_first), flat(conv_second), odd, even, got
    )
    new_conv, new_conv_first, new_conv_second = [x.reshape(conv_weights.shape) for x in new]
    small_grad = jnp.where(first_core, table[0:6], table[6:12])
    new_small, new_small_first, new_small_second = adam_rows(
        small_params, small_first, small_second, (small_grad * clip)[None], rate_small
    )
    return (
        new_conv,
        new_conv_first,
        new_conv_second,
        new_small,
        new_small_first,
        new_small_second,
        loss_sum,
        valid_count,
        grad_norm,
    )


def solution(mesh):
    in_specs = (
        P(None, "band", None, None),
        P(None, "band", None, None),
        P(None, "band", None),
        P("section", None, None, None, None, None),
        P("section", None, None),
        P("section", None, None, None, None, None),
        P("section", None, None, None, None, None),
        P("section", None, None),
        P("section", None, None),
    )
    out_specs = (
        P("section", None, None, None, None, None),
        P("section", None, None, None, None, None),
        P("section", None, None, None, None, None),
        P("section", None, None),
        P("section", None, None),
        P("section", None, None),
        P(),
        P(),
        P(),
    )
    return jax.shard_map(local, mesh=mesh, in_specs=in_specs, out_specs=out_specs, check_vma=False)
```

```python
import functools

import jax
import jax.numpy as jnp
from jax import lax
from jax.experimental import pallas as pl
from jax.experimental.pallas import tpu as pltpu
from jax.sharding import PartitionSpec as P

GROUPS = 32
STEP = 10
PAIR = 2

clip_level = 0.01
rate_conv = 0.02
rate_small = 0.2
adam_eps = 1e-08
decay_rate = 0.01

BF = jnp.bfloat16
F32 = jnp.float32
VM = pl.BlockSpec(memory_space=pltpu.VMEM)
SM = pl.BlockSpec(memory_space=pltpu.SMEM)
HB = pl.BlockSpec(memory_space=pltpu.HBM)


def split(x):
    hi = x.astype(BF)
    return hi, (x - hi.astype(F32)).astype(BF)


def group_sum(row, per):
    lane = lax.broadcasted_iota(jnp.int32, row.shape, 1)
    width = row.shape[1]
    step = 1
    while step < per:
        other = jnp.where(
            (lane // step) % 2 == 0, pltpu.roll(row, width - step, 1), pltpu.roll(row, step, 1)
        )
        row = row + other
        step *= 2
    return row


def sigmoid(u):
    return 0.5 * jnp.tanh(0.5 * u) + 0.5


def tiles_at(ref, at, n):
    return pl.ds(0 if ref.shape[1] == n // 2 else at // 2, n // 2)


def put_tiles(hi_ref, lo_ref, a_ref, at, n):
    _, _, half, c = a_ref.shape
    d = [a_ref[pl.ds(at + t, n // 2, stride=2)] for t in range(4)]
    k = lax.broadcasted_iota(jnp.int32, (n // 2, half, c), 1)
    to = tiles_at(hi_ref, at, n)
    for i, tile in enumerate((d[0] - d[2], d[1] + d[2], d[2] - d[1], d[1] - d[3])):
        even, odd = tile[:, 0], tile[:, 1]
        down = jnp.where(k == 0, 0.0, pltpu.roll(odd, 1, 1))
        up = jnp.where(k == half - 1, 0.0, pltpu.roll(even, half - 1, 1))
        for q, part in enumerate((down, even, odd, up)):
            hi, lo = split(part)
            hi_ref[i, to, :, q * c : (q + 1) * c] = hi
            lo_ref[i, to, :, q * c : (q + 1) * c] = lo


def put_edges(a_ref, side, edge):
    cols = a_ref.shape[0] - 2
    a_ref[0:1] = jnp.where(side == 1, edge, 0.0)
    a_ref[cols + 1 : cols + 2] = jnp.where(side == 0, edge, 0.0)


def tile_of(ref, i, at, n):
    _, _, half, width = ref.shape
    return ref[i, tiles_at(ref, at, n)].reshape(n // 2 * half, width)


def pair_products(hi_ref, lo_ref, whi_ref, wlo_ref, at, n, dot):
    m = []
    for i in range(4):
        hi = tile_of(hi_ref, i, at, n)
        w = whi_ref[i]
        m.append(dot(hi, w) + dot(hi, wlo_ref[i]) + dot(tile_of(lo_ref, i, at, n), w))
    return m[0] + (m[1] + m[2]), (m[1] - m[2]) - m[3]


def pair_rows(one, two):
    return jnp.concatenate(
        [one.sum(0, keepdims=True), two.sum(0, keepdims=True), jnp.zeros((6, one.shape[1]), F32)], 0
    )


def chunk_of(cols, most):
    return max(n for n in range(1, most + 1) if cols % n == 0)


NEAR = 2 << 20


def is_near(x):
    return x.size * 4 <= NEAR


def room_for(field, fields):
    room = 8 if is_near(field) else fields + 1
    return pltpu.CompilerParams(vmem_limit_bytes=room * field.size * 4 + (6 << 20))


def result(shape):
    near = pltpu.VMEM(shape, F32)
    return near if is_near(jax.ShapeDtypeStruct(shape, F32)) else jax.ShapeDtypeStruct(shape, F32)


def held(args):
    return [
        pltpu.with_memory_space_constraint(x, pltpu.VMEM) if x.ndim == 4 and is_near(x) else x
        for x in args
    ]


def far(args):
    return [pltpu.with_memory_space_constraint(x, pltpu.HBM) for x in args]


def fetch(pick, which, sources, into, sem):
    for k, source in enumerate(sources):

        @pl.when(pick == k)
        def _(source=source):
            pltpu.make_async_copy(source.at[which], into, sem).start()


def fetched(which, sources, into, sem):
    pltpu.make_async_copy(sources[0].at[which], into, sem).wait()


def pack(w_ref, hi_ref, lo_ref, flipped):
    c = w_ref.shape[-1]
    zero = jnp.zeros((c, c), BF)
    for a in range(3):
        if flipped:
            g0, g1, g2 = [w_ref[2 - a, 2 - t] for t in range(3)]
        else:
            g0, g1, g2 = [w_ref[a, t] for t in range(3)]
        both, mid = 0.5 * (g0 + g2), 0.5 * g1
        for i, g in enumerate((g0, both + mid, both - mid, g2)):
            hi, lo = split(g)
            for p in range(2):
                q, p = slice((a + p) * c, (a + p + 1) * c), slice(p * c, (p + 1) * c)
                at = (i, p, q) if flipped else (i, q, p)
                hi_ref[at], lo_ref[at] = hi, lo
    for i in range(4):
        for q, p in ((0, 1), (3, 0)):
            q, p = slice(q * c, (q + 1) * c), slice(p * c, (p + 1) * c)
            at = (i, p, q) if flipped else (i, q, p)
            hi_ref[at], lo_ref[at] = zero, zero


RUN = 32
FAR_RUN = 4


def in_turns(unrolled, cols, fill, tiles, ready, conv, carry):
    if not unrolled:
        n = FAR_RUN
        runs = cols // n
        carry = lax.fori_loop(0, runs, lambda j, c: fill(j * n, n, c), carry)
        ready()

        def step(j, carry):
            tiles(j * n, n)
            return conv(j * n, n, carry)

        return lax.fori_loop(0, runs, step, carry)
    n = chunk_of(cols, RUN)
    done = min(cols, n + 2)
    carry = fill(0, done, carry)
    tiles(0, n)
    ready()
    for at in range(0, cols, n):
        carry = conv(at, n, carry)
        more = min(n, cols - done)
        if more > 0:
            carry = fill(done, more, carry)
            done += more
        if at + n < cols:
            tiles(at + n, n)
    return carry


def forward_kernel(sources, following, with_res, *refs):
    refs = list(refs)
    take = lambda n: [refs.pop(0) for _ in range(n)]
    info_ref, next_ref, w_ref, v_ref, in_ref, own_ref, small_ref = take(7)
    res_ref = take(1)[0] if with_res else None
    source_refs = take(sources)
    out_ref, msg_ref, norm_ref, after_ref, a_ref, hi_ref, lo_ref, whi_ref, wlo_ref, sem = refs
    cols, _, half, c = v_ref.shape
    rows = 2 * half
    side = info_ref[0]
    fetch(next_ref[1], following, source_refs, after_ref, sem)
    per = c // GROUPS
    count = float(PAIR * cols * rows * per)
    sums = group_sum(own_ref[rows : rows + 8, :] + in_ref[rows : rows + 8, :], per) / count
    mean = sums[0:1]
    inv = lax.rsqrt(sums[1:2] - mean * mean + 1e-05)
    norm_ref[0:1, :] = mean
    norm_ref[1:2, :] = inv
    norm_ref[2:8, :] = jnp.zeros((6, c), F32)
    gain = inv * small_ref[0:1, :]
    shift = small_ref[1:2, :]
    bias = small_ref[2:3, :]

    def act(x):
        u = (x - mean) * gain + shift
        return u * sigmoid(u)

    put_edges(a_ref, side, act(in_ref[0:rows, :].reshape(1, 2, half, c)))

    def ready():
        pack(w_ref, whi_ref, wlo_ref, False)

    def fill(at, n, carry):
        a_ref[pl.ds(1 + at, n)] = act(v_ref[pl.ds(at, n)])
        return carry

    def tiles(at, n):
        put_tiles(hi_ref, lo_ref, a_ref, at, n)

    def dot(a, b):
        return jnp.dot(a, b, preferred_element_type=F32)

    def conv(at, n, carry):
        one, two = carry
        for t, acc in enumerate(pair_products(hi_ref, lo_ref, whi_ref, wlo_ref, at, n, dot)):
            to = pl.ds(at + t, n // 2, stride=2)
            for p in range(2):
                o = (acc[:, p * c : (p + 1) * c] + bias).reshape(n // 2, half, c)
                if with_res:
                    o = o + res_ref[to, p]
                out_ref[to, p] = o
                f = o.reshape(-1, 8, c)
                one = one + f.sum(0)
                two = two + (f * f).sum(0)
        return one, two

    zero = jnp.zeros((8, c), F32)
    one, two = in_turns(is_near(v_ref), cols, fill, tiles, ready, conv, (zero, zero))
    last = jnp.where(side == 0, cols - 1, 0)
    msg_ref[0:rows, :] = out_ref[pl.ds(last, 1)].reshape(rows, c)
    msg_ref[rows : rows + 8, :] = pair_rows(one, two)
    fetched(following, source_refs, after_ref, sem)


def tile_scratch(cols, half, c, lanes=(4, 4)):
    field = (cols, 2, half, c)
    pairs = (cols if is_near(jax.ShapeDtypeStruct(field, F32)) else FAR_RUN) // 2
    tiles = [pltpu.VMEM((4, pairs, half, width * c), BF) for width in lanes]
    return [pltpu.VMEM((cols + 2, 2, half, c), F32)] + tiles


def conv_scratch(cols, half, c, packed):
    return (
        tile_scratch(cols, half, c) + [pltpu.VMEM(packed, BF)] * 2 + [pltpu.SemaphoreType.DMA(())]
    )


def conv_forward(info, weights, v, msg_in, msg_own, small, res=None):
    cols, _, half, c = v.shape
    rows = 2 * half
    w, sources, (info_next, following) = weights
    args = [info, info_next, w, v, msg_in, msg_own, small] + ([] if res is None else [res])
    pixels = cols * rows
    return pl.pallas_call(
        functools.partial(forward_kernel, len(sources), following, res is not None),
        out_shape=[result(v.shape), result((rows + 8, c)), result((8, c)), result(w.shape)],
        in_specs=[SM, SM] + [VM] * (len(args) - 2) + [HB] * len(sources),
        out_specs=[VM] * 4,
        scratch_shapes=conv_scratch(cols, half, c, (4, 4 * c, 2 * c)),
        compiler_params=room_for(v, 6),
        cost_estimate=pl.CostEstimate(
            flops=pixels * 72 * c * c, bytes_accessed=pixels * c * 8, transcendentals=pixels * c
        ),
    )(*held(args), *far(sources))


def enter_norm(own_ref, in_ref, norm_ref, small_ref, cols, rows):
    c = own_ref.shape[-1]
    per = c // GROUPS
    count = float(PAIR * cols * rows * per)
    gain = small_ref[0:1, :]
    mean = norm_ref[0:1, :]
    inv = norm_ref[1:2, :]
    sums = own_ref[rows : rows + 8, :] + in_ref[rows : rows + 8, :]
    means = group_sum(sums * gain, per) / count
    first, second = means[0:1], means[1:2]

    def enter(t, v):
        return inv * (t * gain - first - (v - mean) * inv * second)

    return enter


def enter_kernel(t_ref, in_ref, own_ref, v_ref, edge_ref, norm_ref, small_ref, g_ref, ge_ref, bias_ref):
    cols, _, half, c = t_ref.shape
    rows = 2 * half
    enter = enter_norm(own_ref, in_ref, norm_ref, small_ref, cols, rows)
    edge = enter(in_ref[0:rows, :], edge_ref[0:rows, :])
    ge_ref[0:rows, :] = edge
    ge_ref[rows : rows + 8, :] = jnp.zeros((8, c), F32)
    n = chunk_of(cols, 8)

    def fill(j, total):
        at = pl.ds(j * n, n)
        g = enter(t_ref[at], v_ref[at])
        g_ref[at] = g
        return total + g.reshape(-1, 8, c).sum(0)

    total = lax.fori_loop(0, cols // n, fill, jnp.zeros((8, c), F32))
    bias_ref[...] = jnp.broadcast_to(total.sum(0, keepdims=True), (8, c))


def norm_enter(t, msg_in, norm):
    cols, _, half, c = t.shape
    return pl.pallas_call(
        enter_kernel,
        out_shape=[
            result(t.shape),
            result((2 * half + 8, c)),
            result((8, c)),
        ],
        in_specs=[VM] * 7,
        out_specs=[VM] * 3,
        compiler_params=room_for(t, 4),
    )(*held([t, msg_in, *norm]))


def backward_kernel(sources, following, with_norm, with_res, *refs):
    refs = list(refs)
    take = lambda n: [refs.pop(0) for _ in range(n)]
    info_ref, next_ref, w_ref, t_ref, in_ref = take(5)
    if with_norm:
        own_ref, vp_ref, vpe_ref, normp_ref, smallp_ref = take(5)
    if with_res:
        res_ref, rese_ref = take(2)
    ve_ref, norme_ref, smalle_ref = take(3)
    source_refs = take(sources)
    if with_norm:
        g_ref, ge_ref = take(2)
    out_ref, msg_ref, bias_ref, after_ref, a_ref, hi_ref, lo_ref, bhi_ref, blo_ref, sem = refs
    cols, _, half, c = t_ref.shape
    rows = 2 * half
    side = info_ref[0]
    fetch(next_ref[1], following, source_refs, after_ref, sem)
    edge = in_ref[0:rows, :]
    if with_norm:
        enter = enter_norm(own_ref, in_ref, normp_ref, smallp_ref, cols, rows)
        edge = enter(edge, vpe_ref[0:rows, :])
        if with_res:
            edge = edge + rese_ref[0:rows, :]
        ge_ref[0:rows, :] = edge
        ge_ref[rows : rows + 8, :] = jnp.zeros((8, c), F32)
    put_edges(a_ref, side, edge.reshape(1, 2, half, c))
    zero = jnp.zeros((8, c), F32)

    def ready():
        pack(w_ref, bhi_ref, blo_ref, True)

    def fill(at, n, carry):
        one, two, total = carry
        run = pl.ds(at, n)
        g = t_ref[run]
        if with_norm:
            g = enter(g, vp_ref[run])
            if with_res:
                g = g + res_ref[run]
            g_ref[run] = g
        a_ref[pl.ds(1 + at, n)] = g
        return one, two, total + g.reshape(-1, 8, c).sum(0)

    gain_e, shift_e = smalle_ref[0:1, :], smalle_ref[1:2, :]
    mean_e, inv_e = norme_ref[0:1, :], norme_ref[1:2, :]

    def dot(a, b):
        return lax.dot_general(a, b, (((1,), (1,)), ((), ())), preferred_element_type=F32)

    def conv(at, n, carry):
        one, two, total = carry
        for k, acc in enumerate(pair_products(hi_ref, lo_ref, bhi_ref, blo_ref, at, n, dot)):
            to = pl.ds(at + k, n // 2, stride=2)
            for p in range(2):
                q = acc[:, p * c : (p + 1) * c].reshape(n // 2, half, c)
                normed = (ve_ref[to, p] - mean_e) * inv_e
                u = normed * gain_e + shift_e
                s = sigmoid(u)
                t = q * (s * (1.0 + u * (1.0 - s)))
                out_ref[to, p] = t
                one = one + t.reshape(-1, 8, c).sum(0)
                two = two + (t * normed).reshape(-1, 8, c).sum(0)
        return one, two, total

    def tiles(at, n):
        put_tiles(hi_ref, lo_ref, a_ref, at, n)

    one, two, total = in_turns(is_near(t_ref), cols, fill, tiles, ready, conv, (zero, zero, zero))
    bias_ref[...] = jnp.broadcast_to(total.sum(0, keepdims=True), (8, c))
    last = jnp.where(side == 0, cols - 1, 0)
    msg_ref[0:rows, :] = out_ref[pl.ds(last, 1)].reshape(rows, c)
    msg_ref[rows : rows + 8, :] = pair_rows(one, two)
    fetched(following, source_refs, after_ref, sem)


def conv_backward(info, weights, t, msg_in, v_e, norm_e, small_e, norm=None, res=None):
    cols, _, half, c = t.shape
    rows = 2 * half
    w, sources, (info_next, following) = weights
    args = [info, info_next, w, t, msg_in] + list(norm or ()) + list(res or ())
    args += [v_e, norm_e, small_e]
    field, msg = result(t.shape), result((rows + 8, c))
    outs = ([field, msg] if norm else []) + [field, msg, result((8, c)), result(w.shape)]
    pixels = cols * rows
    places = {}
    if norm and not is_near(t):
        places = {3: 2, 10: 0} if res else {3: 2}
    got = pl.pallas_call(
        functools.partial(backward_kernel, len(sources), following, norm is not None, res is not None),
        out_shape=outs,
        input_output_aliases=places,
        in_specs=[SM, SM] + [VM] * (len(args) - 2) + [HB] * len(sources),
        out_specs=[VM] * len(outs),
        scratch_shapes=conv_scratch(cols, half, c, (4, 2 * c, 4 * c)),
        compiler_params=room_for(t, 8),
        cost_estimate=pl.CostEstimate(
            flops=pixels * 72 * c * c, bytes_accessed=pixels * c * 16, transcendentals=pixels * c
        ),
    )(*held(args), *far(sources))
    return got if norm else [t, msg_in] + list(got)


def kernel_grad_kernel(with_prev, with_other, *refs):
    refs = list(refs)
    take = lambda n: [refs.pop(0) for _ in range(n)]
    info_ref, v_ref, edge_ref, norm_ref, small_ref, g_ref = take(6)
    prev_ref = take(1)[0] if with_prev else None
    other_ref = take(1)[0] if with_other else None
    out_ref = take(1)[0]
    send_ref = take(1)[0] if with_other else None
    a_ref, hi_ref, lo_ref, ghi_ref, glo_ref = refs
    cols, _, half, c = v_ref.shape
    rows = 2 * half
    mine = info_ref[2] == 1

    @pl.when(jnp.logical_not(mine))
    def _():
        out_ref[...] = prev_ref[...] if with_prev else jnp.zeros_like(out_ref)

    @pl.when(mine)
    def _():
        mean = norm_ref[0:1, :]
        gain = norm_ref[1:2, :] * small_ref[0:1, :]
        shift = small_ref[1:2, :]

        def act(x):
            u = (x - mean) * gain + shift
            return u * sigmoid(u)

        edge = act(edge_ref[0:rows, :].reshape(1, 2, half, c))
        put_edges(a_ref, info_ref[0], edge)

        def fill(at, n, carry):
            run = pl.ds(at, n)
            a_ref[pl.ds(1 + at, n)] = act(v_ref[run])
            return carry

        def tiles(at, n):
            put_tiles(hi_ref, lo_ref, a_ref, at, n)
            even, odd = [g_ref[pl.ds(at + t, n // 2, stride=2)] for t in range(2)]
            to = tiles_at(ghi_ref, at, n)
            for i, tile in enumerate((even, even + odd, even - odd, -odd)):
                for p in range(2):
                    hi, lo = split(tile[:, p])
                    ghi_ref[i, to, :, p * c : (p + 1) * c] = hi
                    glo_ref[i, to, :, p * c : (p + 1) * c] = lo

        def dot(a, b):
            return lax.dot_general(a, b, (((0,), (0,)), ((), ())), preferred_element_type=F32)

        def products(at, n, carry):
            add = not isinstance(at, int) or at > 0
            m = []
            for i in range(4):
                hi, ghi = tile_of(hi_ref, i, at, n), tile_of(ghi_ref, i, at, n)
                acc = dot(hi, ghi) + dot(hi, tile_of(glo_ref, i, at, n)) + dot(tile_of(lo_ref, i, at, n), ghi)
                m.append([acc[a * c : (a + 1) * c, :c] + acc[(a + 1) * c : (a + 2) * c, c:] for a in range(3)])
            for a in range(3):
                both, apart = 0.5 * (m[1][a] + m[2][a]), 0.5 * (m[1][a] - m[2][a])
                for t, new in enumerate((m[0][a] + both, apart, both + m[3][a])):
                    to = slice((a * 3 + t) * c, (a * 3 + t + 1) * c)
                    out_ref[to, :] = out_ref[to, :] + new if add else new
            return carry

        if not is_near(v_ref):
            out_ref[...] = jnp.zeros_like(out_ref)
        in_turns(is_near(v_ref), cols, fill, tiles, lambda: None, products, 0)

    if with_other:
        keep_own = info_ref[0] == 0
        n = 9 * c // 16

        def exchange(j, _):
            at = pl.ds(pl.multiple_of(j * n, 8), n)
            own, other = out_ref[at, :], other_ref[at, :]
            out_ref[at, :] = jnp.where(keep_own, own, other)
            send_ref[at, :] = jnp.where(keep_own, other, own)
            return 0

        lax.fori_loop(0, 16, exchange, 0)


def kernel_grad(info, v, edge, norm, small, g, prev=None, other=None):
    cols, _, half, c = v.shape
    pixels = cols * half * 2
    args = [info, v, edge, norm, small, g] + [x for x in (prev, other) if x is not None]
    outs = [result((9 * c, c))] * (1 if other is None else 2)
    got = pl.pallas_call(
        functools.partial(kernel_grad_kernel, prev is not None, other is not None),
        out_shape=outs,
        in_specs=[SM] + [VM] * (len(args) - 1),
        out_specs=[VM] * len(outs),
        scratch_shapes=tile_scratch(cols, half, c, (4, 4, 2, 2)),
        compiler_params=room_for(v, 6),
        cost_estimate=pl.CostEstimate(
            flops=pixels * 72 * c * c, bytes_accessed=pixels * c * 8, transcendentals=pixels * c
        ),
    )(*held(args))
    return got[0] if other is None else got


def from_rows(ref, at, n, p):
    half = ref.shape[0] // 2
    return jnp.swapaxes(ref[pl.ds(p, half, stride=2), pl.ds(at, n), :], 0, 1)


def arrive_kernel(sources, info_ref, raw_ref, *refs):
    source_refs, (out_ref, msg_ref, after_ref, sem) = refs[:sources], refs[sources:]
    fetch(info_ref[1], 0, source_refs, after_ref, sem)
    rows, cols, c = raw_ref.shape
    one = two = jnp.zeros((8, c), F32)
    run = chunk_of(cols, RUN)
    for at in range(0, cols, run):
        for p in range(2):
            x = from_rows(raw_ref, at, run, p)
            out_ref[at : at + run, p] = x
            f = x.reshape(-1, 8, c)
            one = one + f.sum(0)
            two = two + (f * f).sum(0)
    last = jnp.where(info_ref[0] == 0, cols - 1, 0)
    msg_ref[0:rows, :] = out_ref[pl.ds(last, 1)].reshape(rows, c)
    msg_ref[rows : rows + 8, :] = pair_rows(one, two)
    fetched(0, source_refs, after_ref, sem)


def arrived(info, raw, sources):
    rows, cols, c = raw.shape
    return pl.pallas_call(
        functools.partial(arrive_kernel, len(sources)),
        out_shape=[result((cols, 2, rows // 2, c)), result((rows + 8, c)), result((3, 3, c, c))],
        in_specs=[SM, VM] + [HB] * len(sources),
        out_specs=[VM] * 3,
        scratch_shapes=[pltpu.SemaphoreType.DMA(())],
        compiler_params=room_for(raw, 4),
    )(info, raw, *far(sources))


def loss_kernel(repeats, info_ref, final_ref, raw_ref, g_ref, msg_ref, count_ref, valid_ref):
    cols, _, half, c = final_ref.shape
    rows = 2 * half
    side = info_ref[0]
    count = jnp.zeros((1, c), F32)
    for p in range(2):
        extra = from_rows(raw_ref, cols, 8, p)
        valid_ref[p] = extra[0]
        count = count + extra[1].sum(0, keepdims=True)
    count_ref[...] = jnp.broadcast_to(count, (8, c))
    scale = 1.0 / (count * repeats)
    n = chunk_of(cols, RUN)
    total = jnp.zeros((8, c), F32)
    for at in range(0, cols, n):
        column = (lax.broadcasted_iota(jnp.int32, (n, half, c), 0) + (side * cols + at)).astype(F32)
        for p in range(2):
            diff = final_ref[at : at + n, p] - from_rows(raw_ref, at, n, p)
            square = diff * diff + 1.0
            valid = column < valid_ref[p][None]
            g_ref[at : at + n, p] = jnp.where(valid, diff * lax.rsqrt(square) * scale, 0.0)
            part = jnp.where(valid, jnp.sqrt(square) - 1.0, 0.0)
            total = total + part.reshape(-1, 8, c).sum(0)
    last = jnp.where(side == 0, cols - 1, 0)
    msg_ref[0:rows, :] = g_ref[pl.ds(last, 1)].reshape(rows, c)
    msg_ref[rows : rows + 8, :] = total


def loss_and_gradient(info, final, raw, repeats):
    cols, _, half, c = final.shape
    return pl.pallas_call(
        functools.partial(loss_kernel, repeats),
        out_shape=[result(final.shape), result((2 * half + 8, c)), result((8, c))],
        in_specs=[SM] + [VM] * 2,
        out_specs=[VM] * 3,
        scratch_shapes=[pltpu.VMEM((2, half, c), F32)],
        compiler_params=room_for(final, 5),
    )(info, *held([final]), raw)


def small_call(kernel, info, args, outs):
    total = sum(x.size for x in args) + sum(o.size for o in outs)
    return pl.pallas_call(
        kernel,
        out_shape=[result(o.shape) for o in outs],
        in_specs=[SM] * len(info) + [VM] * len(args),
        out_specs=[VM] * len(outs),
        compiler_params=pltpu.CompilerParams(vmem_limit_bytes=total * 8 + (2 << 20)),
    )(*info, *args)


def like(*shape):
    return jax.ShapeDtypeStruct(shape, F32)


def fold_kernel(by, info_ref, keep_ref, got_ref, out_ref, send_ref):
    n = out_ref.shape[0]
    upper = (info_ref[3] // by) % 2 == 1
    low = keep_ref[0:n, :] + got_ref[0:n, :]
    high = keep_ref[n:, :] + got_ref[n:, :]
    out_ref[...] = jnp.where(upper, high, low)
    send_ref[...] = jnp.where(upper, low, high)


def fold(info, by, keep, got):
    half = like(keep.shape[0] // 2, keep.shape[1])
    return small_call(functools.partial(fold_kernel, by), [info], [keep, got], [half, half])


def meet_kernel(info_ref, keep_ref, got_ref, out_ref, square_ref):
    out = keep_ref[...] + got_ref[...]
    out_ref[...] = out
    square_ref[...] = (out * out).reshape(-1, 8, out.shape[-1]).sum(0)


def meet(info, keep, got):
    return small_call(meet_kernel, [info], [keep, got], [keep, like(8, keep.shape[1])])


def unfold_kernel(by, info_ref, mine_ref, other_ref, out_ref):
    n = mine_ref.shape[0]
    upper = (info_ref[3] // by) % 2 == 1
    mine, other = mine_ref[...], other_ref[...]
    out_ref[0:n, :] = jnp.where(upper, other, mine)
    out_ref[n:, :] = jnp.where(upper, mine, other)


def unfold(info, by, mine, other):
    n, c = mine.shape
    return small_call(functools.partial(unfold_kernel, by), [info], [mine, other], [like(2 * n, c)])[0]


TABLE = 16


def spread_kernel(layers, rows, *refs):
    refs = list(refs)
    take = lambda n: [refs.pop(0) for _ in range(n)]
    infos = take(layers)
    parts_ref, square_ref, loss_ref = take(3)
    small = [0.0] * PAIR
    for l in range(layers):
        one_ref, bias1_ref, two_ref, bias2_ref = take(4)
        row = []
        for sums_ref, bias_ref in ((one_ref, bias1_ref), (two_ref, bias2_ref)):
            row += [sums_ref[rows + 1 : rows + 2, :], sums_ref[rows : rows + 1, :], bias_ref[0:1, :]]
        small[l % PAIR] += jnp.where(infos[l][2] == 1, jnp.concatenate(row, 0), 0.0)
    out_ref = take(1)[0]
    bands, n, c = parts_ref.shape
    share = parts_ref[...].sum(0)
    squares = square_ref[...].sum(0, keepdims=True) + (share * share).sum(0, keepdims=True)
    loss = loss_ref[rows : rows + 8, :].sum(0, keepdims=True)
    table = jnp.concatenate(small + [loss, squares, jnp.zeros((2, c), F32)], 0)
    for b in range(bands):
        out_ref[b, 0:n, :] = share
        out_ref[b, n : n + TABLE, :] = table


def spread(infos, rows, parts, square, loss, pieces):
    bands, n, c = parts.shape
    args = [parts, square, loss] + [x for piece in pieces for x in piece]
    kernel = functools.partial(spread_kernel, len(infos), rows)
    return small_call(kernel, infos, args, [like(bands, n + TABLE, c)])[0]


def table_kernel(info_ref, rest_ref, out_ref):
    out_ref[...] = rest_ref[:, rest_ref.shape[1] - TABLE :, :].sum(0)


def adam_step(w, first, second, grad, rate):
    first = 0.5 * first + 0.5 * grad
    second = 0.5 * second + 0.5 * grad * grad
    fix = 1.0 - 0.5**STEP
    step = first / fix / (jnp.sqrt(second / fix) + adam_eps) + decay_rate * w
    return w - rate * step, first, second


def tree_sum(items):
    while len(items) > 1:
        items = [a + b for a, b in zip(items[::2], items[1::2])]
    return items[0]


def adam_kernel(repeats, sections, *refs):
    refs = list(refs)
    take = lambda n: [refs.pop(0) for _ in range(n)]
    info_ref = take(1)[0]
    tables = [ref[...] for ref in take(sections)]
    rest_ref, got_rest_ref, odd_ref, got_odd_ref = take(4)
    small_refs = take(3)
    from_refs = take(3)
    new_small_refs = take(3)
    scalar_ref = take(1)[0]
    to_refs, old_refs, new_refs = take(3), take(3), take(3)
    in_sem, out_sem = refs
    bands = rest_ref.shape[0]
    n = from_refs[0].shape[1] // bands
    runs = [(which, run) for which in range(2) for run in range(bands)]

    def copies(sources, targets, sem, which, run):
        at = pl.ds(run * n, n)
        return [
            pltpu.make_async_copy(a.at[which, at], b.at[which, at], sem.at[k, which, run])
            for k, (a, b) in enumerate(zip(sources, targets))
        ]

    for which, run in runs:
        for copy in copies(from_refs, old_refs, in_sem, which, run):
            copy.start()
    chips = [tables[k] + tables[k + 1] for k in range(0, sections, PAIR)]
    squares = [jnp.sum(t[0:12] * t[0:12]) + jnp.sum(t[13:14]) for t in chips]
    norm = jnp.sqrt(jnp.full((8, 128), tree_sum(squares), F32))
    clip = clip_level / jnp.maximum(norm, clip_level)
    loss = jnp.full((8, 128), jnp.sum(chips[0][12:13]), F32) / repeats
    scalar_ref[0:8, :] = norm
    scalar_ref[8:16, :] = loss
    clip = clip[0:1, 0:1]
    first_core = info_ref[0] == 0
    grad = jnp.where(first_core, chips[0][0:6], chips[0][6:12]) * clip
    new = adam_step(*[ref[...] for ref in small_refs], grad, rate_small)
    for ref, value in zip(new_small_refs, new):
        ref[...] = value
    for which, run in runs:
        for copy in copies(from_refs, old_refs, in_sem, which, run):
            copy.wait()
        at = slice(run * n, (run + 1) * n)
        if which == 0:
            grad = jnp.where(first_core, rest_ref[run, 0:n, :], got_odd_ref[at, :])
        else:
            grad = jnp.where(first_core, got_rest_ref[run, 0:n, :], odd_ref[at, :])
        new = adam_step(*[ref[which, at, :] for ref in old_refs], grad * clip, rate_conv)
        for ref, value in zip(new_refs, new):
            ref[which, at, :] = value
        for copy in copies(new_refs, to_refs, out_sem, which, run):
            copy.start()
    for which, run in runs:
        for copy in copies(new_refs, to_refs, out_sem, which, run):
            copy.wait()


def optimizer(info, repeats, tables, rest, got_rest, odd, got_odd, smalls, states):
    shape, bands = states[0].shape, rest.shape[0]
    args = [*tables, rest, got_rest, odd, got_odd, *smalls]
    sems = pltpu.SemaphoreType.DMA((3, 2, bands))
    return pl.pallas_call(
        functools.partial(adam_kernel, repeats, len(tables)),
        out_shape=[like(*x.shape) for x in smalls] + [like(16, 128)] + [pltpu.HBM(shape, F32)] * 3,
        in_specs=[SM] + [VM] * len(args) + [HB] * 3,
        out_specs=[VM] * 4 + [HB] * 3,
        scratch_shapes=[pltpu.VMEM(shape, F32)] * 6 + [sems] * 2,
        compiler_params=pltpu.CompilerParams(vmem_limit_bytes=11 * states[0].size * 4),
    )(info, *args, *far(states))


def partner(x):
    return lax.ppermute(x, "section", [(i, i ^ 1) for i in range(lax.axis_size("section"))])


def to_image(bands, repeats):
    bands = jnp.repeat(bands, repeats, 0) if repeats > 1 else bands
    got = lax.all_to_all(bands, "band", 0, 0, tiled=True)
    return got.reshape(-1, *got.shape[2:])


def crossed(x, by):
    return lax.ppermute(x, "band", [(i, i ^ by) for i in range(lax.axis_size("band"))])


def band_bits():
    return [1 << k for k in range(lax.axis_size("band").bit_length() - 1)]


def swapped(parts):
    return lax.all_to_all(parts, "band", 0, 0, tiled=True)


def local(
    images,
    targets,
    masks,
    conv_weights,
    small_params,
    conv_first,
    conv_second,
    small_first,
    small_second,
):
    sections = lax.axis_size("section")
    bands = lax.axis_size("band")
    here = lax.axis_index("section")
    core = here % PAIR
    chip = here // PAIR
    chips = sections // PAIR
    layers = sections
    micro, part, width, c = images.shape
    repeats = bands // micro
    cols = width // PAIR
    rows = part * bands
    half = rows // 2

    image = to_image(lax.dynamic_slice_in_dim(images, core * cols, cols, 2), repeats)
    lengths = jnp.sum(masks.astype(F32), 2)
    counts = jnp.where(jnp.arange(part)[None, :] == 0, jnp.sum(lengths), 0.0)
    extra = jnp.stack([lengths, jnp.broadcast_to(counts, lengths.shape)] + [jnp.zeros_like(lengths)] * 6, 2)
    extra = jnp.broadcast_to(extra[..., None], (micro, part, 8, c))
    target = jnp.concatenate([lax.dynamic_slice_in_dim(targets, core * cols, cols, 2), extra], 2)
    image, target = lax.optimization_barrier((image, target))
    target = to_image(target, repeats)

    own = (conv_weights[0], jnp.pad(small_params[0], ((0, 2), (0, 0))))
    sources, smalls = [], []
    for k in range(chips):
        shift = [((i + PAIR * k) % sections, i) for i in range(sections)]
        theirs = own if k == 0 else tuple(lax.ppermute(x, "section", shift) for x in own)
        others = tuple(partner(x) for x in theirs)
        sources += [theirs[0], others[0]]
        smalls += [theirs[1], others[1]]
    smalls = jnp.stack(smalls)

    def pick_of(layer):
        return PAIR * ((layer // PAIR - chip) % chips) + (layer % PAIR != core).astype(jnp.int32)

    def info_of(layer):
        mine = (chip == layer // PAIR).astype(jnp.int32)
        return jnp.stack([core, pick_of(layer), mine, lax.axis_index("band")]).astype(jnp.int32)

    def norms_of(layer):
        both = lax.dynamic_index_in_dim(smalls, pick_of(layer), 0, False)
        return jnp.pad(both[0:3], ((0, 5), (0, 0))), jnp.pad(both[3:6], ((0, 5), (0, 0)))

    infos = [info_of(l) for l in range(layers)]
    norms = [norms_of(l) for l in range(layers)]
    image, infos, norms = lax.optimization_barrier((image, infos, norms))
    again_first = not is_near(jax.ShapeDtypeStruct((cols, rows, c), F32))
    order = [(l, k) for l in range(layers) for k in range(2)]
    for l in reversed(range(layers)):
        order += [(l, 0)] * again_first + [(l, 1), (l, 0)]
    order = [(infos[l], k) for l, k in order[1:]] + [(infos[0], 0)]

    def with_next(w):
        return w, sources, order.pop(0)

    field, message, w = arrived(infos[0], image, sources)
    stack = []
    for l in range(layers):
        got = partner(message)
        mid, sent, norm, w = conv_forward(infos[l], with_next(w), field, got, message, norms[l][0])
        again = partner(sent)
        one, first_in = (field, got, norm), (field, got, message, norms[l][0])
        field, message, norm, w = conv_forward(
            infos[l], with_next(w), mid, again, sent, norms[l][1], field
        )
        stack.append((one, (None if again_first else mid, again, norm), first_in))

    def second_back(l, w, t, got, enter, res):
        _, (v2, e2, n2), first_in = stack[l]
        if again_first:
            t, first_in = lax.optimization_barrier((t, first_in))
            v2, _, _, w = conv_forward(infos[l], with_next(w), *first_in)
        grad, grad_edge, t, sent, bias, w = conv_backward(
            infos[l], with_next(w), t, got, v2, n2, norms[l][1], norm=enter, res=res
        )
        return w, t, partner(sent), bias, (sent, v2, e2, n2, norms[l][1]), (grad, grad_edge)

    def grad_of(l, k, v, g, prev, other=None):
        _, edge, norm = stack[l][k]
        return kernel_grad(infos[l], v, edge, norm, norms[l][k], g, prev, other)

    grad, message, count = loss_and_gradient(infos[0], field, target, repeats)
    got = partner(message)
    loss_message = message

    t, enter, res = grad, None, None
    slots = [[None, None] for _ in range(PAIR)]
    pieces = {}
    for l in reversed(range(1, layers)):
        slot = slots[l % PAIR]
        w, t, got, bias2, enter, res = second_back(l, w, t, got, enter, res)
        k2 = grad_of(l, 1, enter[1], res[0], slot[1])
        sent = enter[0]
        v1, e1, n1 = stack[l][0]
        mid, _, t, message, bias1, w = conv_backward(
            infos[l], with_next(w), t, got, v1, n1, norms[l][0], norm=enter
        )
        got = partner(message)
        k1 = grad_of(l, 0, v1, mid, slot[0], k2 if l == 1 else None)
        enter = (message, v1, e1, n1, norms[l][0])
        slot[:] = [k1, k2]
        pieces[l] = (message, bias1, sent, bias2)

    keep, send = slots[1][0]
    info, bits = infos[0], band_bits()
    keep, send = fold(info, bits[0], keep, partner(send))
    got_odd = crossed(send, bits[0])
    w, t, got, bias2, enter, res = second_back(0, w, t, got, enter, res)
    mid, got_odd = lax.optimization_barrier((res[0], got_odd))
    keep, send = fold(info, bits[1], keep, got_odd)
    got_odd = crossed(send, bits[1])
    k2 = grad_of(0, 1, enter[1], mid, slots[0][1])
    t, k2, got_odd = lax.optimization_barrier((t, k2, got_odd))
    for by in bits[2:-1]:
        keep, send = fold(info, by, keep, got_odd)
        got_odd = crossed(send, by)
    keep, send = fold(info, bits[-1], keep, got_odd)
    mid, mid_edge, bias1 = norm_enter(t, got, enter)
    mid, send = lax.optimization_barrier((mid, send))
    got_odd = crossed(send, bits[-1])
    sent = enter[0]
    v1, e1, n1 = stack[0][0]
    even, send = grad_of(0, 0, v1, mid, slots[0][0], k2)
    even = meet(info, even, partner(send))[0]
    mid, even, got_odd = lax.optimization_barrier((mid, even, got_odd))
    odd, odd_square = meet(info, keep, got_odd)
    odd_got = crossed(odd, bits[-1])
    parts = swapped(even.reshape(bands, -1, c))
    _, _, _, message, _, _ = conv_backward(
        info, with_next(w), mid, mid_edge, v1, n1, norms[0][0]
    )
    pieces[0] = (message, bias1, sent, bias2)
    message, odd_got = lax.optimization_barrier((message, odd_got))
    odd = unfold(info, bits[-1], odd, odd_got)
    odd_got = crossed(odd, bits[-2])
    parts, odd_got = lax.optimization_barrier((parts, odd_got))
    odd = unfold(info, bits[-2], odd, odd_got)
    for by in bits[-3::-1]:
        odd = unfold(info, by, odd, crossed(odd, by))
    got_odd = partner(odd)
    rest = spread(infos, rows, parts, odd_square, loss_message, [pieces[l] for l in range(layers)])
    rest = swapped(rest)
    table = small_call(table_kernel, [info], [rest], [like(TABLE, c)])[0]
    got_rest = partner(rest)
    tables = [table]
    for by in range(1, sections):
        tables.append(lax.ppermute(table, "section", [(i, i ^ by) for i in range(sections)]))

    flat = lambda x: x.reshape(2, 9 * c, c)
    smalls = [x[0] for x in (small_params, small_first, small_second)]
    states = [flat(x) for x in (conv_weights, conv_first, conv_second)]
    *new_smalls, scalars, new_conv, new_conv_first, new_conv_second = optimizer(
        info, repeats, tables, rest, got_rest, odd, got_odd, smalls, states
    )
    new_conv, new_conv_first, new_conv_second = [
        x.reshape(conv_weights.shape) for x in (new_conv, new_conv_first, new_conv_second)
    ]
    new_small, new_small_first, new_small_second = [x[None] for x in new_smalls]
    grad_norm, loss_sum, valid_count = scalars[0, 0], scalars[8, 0], count[0, 0]
    return (
        new_conv,
        new_conv_first,
        new_conv_second,
        new_small,
        new_small_first,
        new_small_second,
        loss_sum,
        valid_count,
        grad_norm,
    )


def solution(mesh):
    in_specs = (
        P(None, "band", None, None),
        P(None, "band", None, None),
        P(None, "band", None),
        P("section", None, None, None, None, None),
        P("section", None, None),
        P("section", None, None, None, None, None),
        P("section", None, None, None, None, None),
        P("section", None, None),
        P("section", None, None),
    )
    out_specs = (
        P("section", None, None, None, None, None),
        P("section", None, None, None, None, None),
        P("section", None, None, None, None, None),
        P("section", None, None),
        P("section", None, None),
        P("section", None, None),
        P(),
        P(),
        P(),
    )
    return jax.shard_map(local, mesh=mesh, in_specs=in_specs, out_specs=out_specs, check_vma=False)
```

```python
import functools

import jax
import jax.numpy as jnp
from jax import lax
from jax.experimental import pallas as pl
from jax.experimental.pallas import tpu as pltpu
from jax.sharding import PartitionSpec as P

GROUPS = 32
STEP = 10
PAIR = 2

clip_level = 0.01
rate_conv = 0.02
rate_small = 0.2
adam_eps = 1e-08
decay_rate = 0.01

BF = jnp.bfloat16
F32 = jnp.float32
VM = pl.BlockSpec(memory_space=pltpu.VMEM)
SM = pl.BlockSpec(memory_space=pltpu.SMEM)
HB = pl.BlockSpec(memory_space=pltpu.HBM)


def split(x):
    hi = x.astype(BF)
    return hi, (x - hi.astype(F32)).astype(BF)


def group_sum(row, per):
    lane = lax.broadcasted_iota(jnp.int32, row.shape, 1)
    width = row.shape[1]
    step = 1
    while step < per:
        other = jnp.where(
            (lane // step) % 2 == 0, pltpu.roll(row, width - step, 1), pltpu.roll(row, step, 1)
        )
        row = row + other
        step *= 2
    return row


def sigmoid(u):
    return 0.5 * jnp.tanh(0.5 * u) + 0.5


def tiles_at(ref, at, n):
    return pl.ds(0 if ref.shape[1] == n // 2 else at // 2, n // 2)


def put_tiles(hi_ref, lo_ref, a_ref, at, n):
    _, _, half, c = a_ref.shape
    d = [a_ref[pl.ds(at + t, n // 2, stride=2)] for t in range(4)]
    k = lax.broadcasted_iota(jnp.int32, (n // 2, half, c), 1)
    to = tiles_at(hi_ref, at, n)
    for i, tile in enumerate((d[0] - d[2], d[1] + d[2], d[2] - d[1], d[1] - d[3])):
        even, odd = tile[:, 0], tile[:, 1]
        down = jnp.where(k == 0, 0.0, pltpu.roll(odd, 1, 1))
        up = jnp.where(k == half - 1, 0.0, pltpu.roll(even, half - 1, 1))
        for q, part in enumerate((down, even, odd, up)):
            hi, lo = split(part)
            hi_ref[i, to, :, q * c : (q + 1) * c] = hi
            lo_ref[i, to, :, q * c : (q + 1) * c] = lo


def put_edges(a_ref, side, edge):
    cols = a_ref.shape[0] - 2
    a_ref[0:1] = jnp.where(side == 1, edge, 0.0)
    a_ref[cols + 1 : cols + 2] = jnp.where(side == 0, edge, 0.0)


def tile_of(ref, i, at, n):
    _, _, half, width = ref.shape
    return ref[i, tiles_at(ref, at, n)].reshape(n // 2 * half, width)


def pair_products(hi_ref, lo_ref, whi_ref, wlo_ref, at, n, dot):
    m = []
    for i in range(4):
        hi = tile_of(hi_ref, i, at, n)
        w = whi_ref[i]
        m.append(dot(hi, w) + dot(hi, wlo_ref[i]) + dot(tile_of(lo_ref, i, at, n), w))
    return m[0] + (m[1] + m[2]), (m[1] - m[2]) - m[3]


def pair_rows(one, two):
    return jnp.concatenate(
        [one.sum(0, keepdims=True), two.sum(0, keepdims=True), jnp.zeros((6, one.shape[1]), F32)], 0
    )


def chunk_of(cols, most):
    return max(n for n in range(1, most + 1) if cols % n == 0)


NEAR = 2 << 20


def is_near(x):
    return x.size * 4 <= NEAR


def room_for(field, fields):
    room = 8 if is_near(field) else fields + 1
    return pltpu.CompilerParams(vmem_limit_bytes=room * field.size * 4 + (6 << 20))


def result(shape):
    near = pltpu.VMEM(shape, F32)
    return near if is_near(jax.ShapeDtypeStruct(shape, F32)) else jax.ShapeDtypeStruct(shape, F32)


def held(args):
    return [
        pltpu.with_memory_space_constraint(x, pltpu.VMEM) if x.ndim == 4 and is_near(x) else x
        for x in args
    ]


def far(args):
    return [pltpu.with_memory_space_constraint(x, pltpu.HBM) for x in args]


def fetch(pick, which, sources, into, sem):
    for k, source in enumerate(sources):

        @pl.when(pick == k)
        def _(source=source):
            pltpu.make_async_copy(source.at[which], into, sem).start()


def fetched(which, sources, into, sem):
    pltpu.make_async_copy(sources[0].at[which], into, sem).wait()


def pack(w_ref, hi_ref, lo_ref, flipped):
    c = w_ref.shape[-1]
    zero = jnp.zeros((c, c), BF)
    for a in range(3):
        if flipped:
            g0, g1, g2 = [w_ref[2 - a, 2 - t] for t in range(3)]
        else:
            g0, g1, g2 = [w_ref[a, t] for t in range(3)]
        both, mid = 0.5 * (g0 + g2), 0.5 * g1
        for i, g in enumerate((g0, both + mid, both - mid, g2)):
            hi, lo = split(g)
            for p in range(2):
                q, p = slice((a + p) * c, (a + p + 1) * c), slice(p * c, (p + 1) * c)
                at = (i, p, q) if flipped else (i, q, p)
                hi_ref[at], lo_ref[at] = hi, lo
    for i in range(4):
        for q, p in ((0, 1), (3, 0)):
            q, p = slice(q * c, (q + 1) * c), slice(p * c, (p + 1) * c)
            at = (i, p, q) if flipped else (i, q, p)
            hi_ref[at], lo_ref[at] = zero, zero


RUN = 32
FAR_RUN = 4


def in_turns(unrolled, cols, fill, tiles, ready, conv, carry):
    if not unrolled:
        n = FAR_RUN
        runs = cols // n
        carry = lax.fori_loop(0, runs, lambda j, c: fill(j * n, n, c), carry)
        ready()

        def step(j, carry):
            tiles(j * n, n)
            return conv(j * n, n, carry)

        return lax.fori_loop(0, runs, step, carry)
    n = chunk_of(cols, RUN)
    done = min(cols, n + 2)
    carry = fill(0, done, carry)
    tiles(0, n)
    ready()
    for at in range(0, cols, n):
        carry = conv(at, n, carry)
        more = min(n, cols - done)
        if more > 0:
            carry = fill(done, more, carry)
            done += more
        if at + n < cols:
            tiles(at + n, n)
    return carry


def from_rows(ref, at, n, p):
    half = ref.shape[0] // 2
    return jnp.swapaxes(ref[pl.ds(p, half, stride=2), pl.ds(at, n), :], 0, 1)


def target_of(ref, at, n, p):
    if isinstance(at, int):
        x = from_rows(ref, at, n, p)
    else:
        wide = from_rows(ref, pl.multiple_of(at // 8 * 8, 8), 8, p)
        x = jnp.where(at % 8 == 0, wide[:n], wide[8 - n :])
    x = x.reshape(n // 2, 2, *x.shape[1:])
    return x[:, 0], x[:, 1]


def forward_kernel(sources, following, with_res, repeats, *refs):
    refs = list(refs)
    take = lambda n: [refs.pop(0) for _ in range(n)]
    info_ref, next_ref, w_ref, v_ref, in_ref, own_ref, small_ref = take(7)
    res_ref = take(1)[0] if with_res else None
    goal_ref = take(1)[0] if repeats else None
    source_refs = take(sources)
    if repeats:
        count_ref = refs.pop(4)
        raw_ref, raw_sem = refs.pop(), refs.pop()
        goal = pltpu.make_async_copy(goal_ref, raw_ref, raw_sem)
        goal.start()
    out_ref, msg_ref, norm_ref, after_ref, a_ref, hi_ref, lo_ref, whi_ref, wlo_ref, sem = refs
    cols, _, half, c = v_ref.shape
    rows = 2 * half
    side = info_ref[0]
    fetch(next_ref[1], following, source_refs, after_ref, sem)
    per = c // GROUPS
    count = float(PAIR * cols * rows * per)
    sums = group_sum(own_ref[rows : rows + 8, :] + in_ref[rows : rows + 8, :], per) / count
    mean = sums[0:1]
    inv = lax.rsqrt(sums[1:2] - mean * mean + 1e-05)
    norm_ref[0:1, :] = mean
    norm_ref[1:2, :] = inv
    norm_ref[2:8, :] = jnp.zeros((6, c), F32)
    gain = inv * small_ref[0:1, :]
    shift = small_ref[1:2, :]
    bias = small_ref[2:3, :]

    def act(x):
        u = (x - mean) * gain + shift
        return u * sigmoid(u)

    put_edges(a_ref, side, act(in_ref[0:rows, :].reshape(1, 2, half, c)))

    lengths = []

    def ready():
        pack(w_ref, whi_ref, wlo_ref, False)
        if repeats:
            goal.wait()
            count = jnp.zeros((1, c), F32)
            for p in range(2):
                extra = from_rows(raw_ref, cols, 8, p)
                lengths.append(extra[0])
                count = count + extra[1].sum(0, keepdims=True)
            count_ref[...] = jnp.broadcast_to(count, (8, c))

    def fill(at, n, carry):
        a_ref[pl.ds(1 + at, n)] = act(v_ref[pl.ds(at, n)])
        return carry

    def tiles(at, n):
        put_tiles(hi_ref, lo_ref, a_ref, at, n)

    def dot(a, b):
        return jnp.dot(a, b, preferred_element_type=F32)

    def conv(at, n, carry):
        one, two = carry
        if repeats:
            scale = 1.0 / (count_ref[0:1, :] * repeats)
            target = [target_of(raw_ref, at, n, p) for p in range(2)]
        for t, acc in enumerate(pair_products(hi_ref, lo_ref, whi_ref, wlo_ref, at, n, dot)):
            to = pl.ds(at + t, n // 2, stride=2)
            for p in range(2):
                o = (acc[:, p * c : (p + 1) * c] + bias).reshape(n // 2, half, c)
                if with_res:
                    o = o + res_ref[to, p]
                if repeats:
                    pair = lax.broadcasted_iota(jnp.int32, o.shape, 0)
                    valid = (side * cols + at + t + 2 * pair).astype(F32) < lengths[p][None]
                    diff = o - target[p][t]
                    square = diff * diff + 1.0
                    out_ref[to, p] = jnp.where(valid, diff * lax.rsqrt(square) * scale, 0.0)
                    part = jnp.where(valid, jnp.sqrt(square) - 1.0, 0.0)
                    one = one + part.reshape(-1, 8, c).sum(0)
                    continue
                out_ref[to, p] = o
                f = o.reshape(-1, 8, c)
                one = one + f.sum(0)
                two = two + (f * f).sum(0)
        return one, two

    zero = jnp.zeros((8, c), F32)
    one, two = in_turns(is_near(v_ref), cols, fill, tiles, ready, conv, (zero, zero))
    last = jnp.where(side == 0, cols - 1, 0)
    msg_ref[0:rows, :] = out_ref[pl.ds(last, 1)].reshape(rows, c)
    msg_ref[rows : rows + 8, :] = pair_rows(one, two)
    fetched(following, source_refs, after_ref, sem)


def tile_scratch(cols, half, c, lanes=(4, 4)):
    field = (cols, 2, half, c)
    pairs = (cols if is_near(jax.ShapeDtypeStruct(field, F32)) else FAR_RUN) // 2
    tiles = [pltpu.VMEM((4, pairs, half, width * c), BF) for width in lanes]
    return [pltpu.VMEM((cols + 2, 2, half, c), F32)] + tiles


def conv_scratch(cols, half, c, packed):
    return (
        tile_scratch(cols, half, c) + [pltpu.VMEM(packed, BF)] * 2 + [pltpu.SemaphoreType.DMA(())]
    )


def conv_forward(info, weights, v, msg_in, msg_own, small, res=None, raw=None, repeats=0):
    cols, _, half, c = v.shape
    rows = 2 * half
    w, sources, (info_next, following) = weights
    args = [info, info_next, w, v, msg_in, msg_own, small] + ([] if res is None else [res])
    distant = ([] if raw is None else [raw]) + sources
    goal = [] if raw is None else [pltpu.SemaphoreType.DMA(()), pltpu.VMEM(raw.shape, F32)]
    pixels = cols * rows
    return pl.pallas_call(
        functools.partial(forward_kernel, len(sources), following, res is not None, repeats),
        out_shape=[result(v.shape), result((rows + 8, c)), result((8, c)), result(w.shape)]
        + [result((8, c))] * bool(repeats),
        in_specs=[SM, SM] + [VM] * (len(args) - 2) + [HB] * len(distant),
        out_specs=[VM] * (5 if repeats else 4),
        scratch_shapes=conv_scratch(cols, half, c, (4, 4 * c, 2 * c)) + goal,
        compiler_params=room_for(v, 7 if repeats else 6),
        cost_estimate=pl.CostEstimate(
            flops=pixels * 72 * c * c, bytes_accessed=pixels * c * 8, transcendentals=pixels * c
        ),
    )(*held(args), *far(distant))


def enter_norm(own_ref, in_ref, norm_ref, small_ref, cols, rows):
    c = own_ref.shape[-1]
    per = c // GROUPS
    count = float(PAIR * cols * rows * per)
    gain = small_ref[0:1, :]
    mean = norm_ref[0:1, :]
    inv = norm_ref[1:2, :]
    sums = own_ref[rows : rows + 8, :] + in_ref[rows : rows + 8, :]
    means = group_sum(sums * gain, per) / count
    first, second = means[0:1], means[1:2]

    def enter(t, v):
        return inv * (t * gain - first - (v - mean) * inv * second)

    return enter


def enter_kernel(t_ref, in_ref, own_ref, v_ref, edge_ref, norm_ref, small_ref, g_ref, ge_ref, bias_ref):
    cols, _, half, c = t_ref.shape
    rows = 2 * half
    enter = enter_norm(own_ref, in_ref, norm_ref, small_ref, cols, rows)
    edge = enter(in_ref[0:rows, :], edge_ref[0:rows, :])
    ge_ref[0:rows, :] = edge
    ge_ref[rows : rows + 8, :] = jnp.zeros((8, c), F32)
    n = chunk_of(cols, 8)

    def fill(j, total):
        at = pl.ds(j * n, n)
        g = enter(t_ref[at], v_ref[at])
        g_ref[at] = g
        return total + g.reshape(-1, 8, c).sum(0)

    total = lax.fori_loop(0, cols // n, fill, jnp.zeros((8, c), F32))
    bias_ref[...] = jnp.broadcast_to(total.sum(0, keepdims=True), (8, c))


def norm_enter(t, msg_in, norm):
    cols, _, half, c = t.shape
    return pl.pallas_call(
        enter_kernel,
        out_shape=[
            result(t.shape),
            result((2 * half + 8, c)),
            result((8, c)),
        ],
        in_specs=[VM] * 7,
        out_specs=[VM] * 3,
        compiler_params=room_for(t, 4),
    )(*held([t, msg_in, *norm]))


def backward_kernel(sources, following, with_norm, with_res, info_ref, *refs):
    @pl.when(info_ref[4] == 1)
    def _():
        backward_body(sources, following, with_norm, with_res, info_ref, *refs)


def backward_body(sources, following, with_norm, with_res, *refs):
    refs = list(refs)
    take = lambda n: [refs.pop(0) for _ in range(n)]
    info_ref, next_ref, w_ref, t_ref, in_ref = take(5)
    if with_norm:
        own_ref, vp_ref, vpe_ref, normp_ref, smallp_ref = take(5)
    if with_res:
        res_ref, rese_ref = take(2)
    ve_ref, norme_ref, smalle_ref = take(3)
    source_refs = take(sources)
    if with_norm:
        g_ref, ge_ref = take(2)
    out_ref, msg_ref, bias_ref, after_ref, a_ref, hi_ref, lo_ref, bhi_ref, blo_ref, sem = refs
    cols, _, half, c = t_ref.shape
    rows = 2 * half
    side = info_ref[0]
    fetch(next_ref[1], following, source_refs, after_ref, sem)
    edge = in_ref[0:rows, :]
    if with_norm:
        enter = enter_norm(own_ref, in_ref, normp_ref, smallp_ref, cols, rows)
        edge = enter(edge, vpe_ref[0:rows, :])
        if with_res:
            edge = edge + rese_ref[0:rows, :]
        ge_ref[0:rows, :] = edge
        ge_ref[rows : rows + 8, :] = jnp.zeros((8, c), F32)
    put_edges(a_ref, side, edge.reshape(1, 2, half, c))
    zero = jnp.zeros((8, c), F32)

    def ready():
        pack(w_ref, bhi_ref, blo_ref, True)

    def fill(at, n, carry):
        one, two, total = carry
        run = pl.ds(at, n)
        g = t_ref[run]
        if with_norm:
            g = enter(g, vp_ref[run])
            if with_res:
                g = g + res_ref[run]
            g_ref[run] = g
        a_ref[pl.ds(1 + at, n)] = g
        return one, two, total + g.reshape(-1, 8, c).sum(0)

    gain_e, shift_e = smalle_ref[0:1, :], smalle_ref[1:2, :]
    mean_e, inv_e = norme_ref[0:1, :], norme_ref[1:2, :]

    def dot(a, b):
        return lax.dot_general(a, b, (((1,), (1,)), ((), ())), preferred_element_type=F32)

    def conv(at, n, carry):
        one, two, total = carry
        for k, acc in enumerate(pair_products(hi_ref, lo_ref, bhi_ref, blo_ref, at, n, dot)):
            to = pl.ds(at + k, n // 2, stride=2)
            for p in range(2):
                q = acc[:, p * c : (p + 1) * c].reshape(n // 2, half, c)
                normed = (ve_ref[to, p] - mean_e) * inv_e
                u = normed * gain_e + shift_e
                s = sigmoid(u)
                t = q * (s * (1.0 + u * (1.0 - s)))
                out_ref[to, p] = t
                one = one + t.reshape(-1, 8, c).sum(0)
                two = two + (t * normed).reshape(-1, 8, c).sum(0)
        return one, two, total

    def tiles(at, n):
        put_tiles(hi_ref, lo_ref, a_ref, at, n)

    one, two, total = in_turns(is_near(t_ref), cols, fill, tiles, ready, conv, (zero, zero, zero))
    bias_ref[...] = jnp.broadcast_to(total.sum(0, keepdims=True), (8, c))
    last = jnp.where(side == 0, cols - 1, 0)
    msg_ref[0:rows, :] = out_ref[pl.ds(last, 1)].reshape(rows, c)
    msg_ref[rows : rows + 8, :] = pair_rows(one, two)
    fetched(following, source_refs, after_ref, sem)


def conv_backward(info, weights, t, msg_in, v_e, norm_e, small_e, norm=None, res=None):
    cols, _, half, c = t.shape
    rows = 2 * half
    w, sources, (info_next, following) = weights
    args = [info, info_next, w, t, msg_in] + list(norm or ()) + list(res or ())
    args += [v_e, norm_e, small_e]
    field, msg = result(t.shape), result((rows + 8, c))
    outs = ([field, msg] if norm else []) + [field, msg, result((8, c)), result(w.shape)]
    pixels = cols * rows
    places = {}
    if norm and not is_near(t):
        places = {3: 2, 10: 0} if res else {3: 2}
    got = pl.pallas_call(
        functools.partial(backward_kernel, len(sources), following, norm is not None, res is not None),
        out_shape=outs,
        input_output_aliases=places,
        in_specs=[SM, SM] + [VM] * (len(args) - 2) + [HB] * len(sources),
        out_specs=[VM] * len(outs),
        scratch_shapes=conv_scratch(cols, half, c, (4, 2 * c, 4 * c)),
        compiler_params=room_for(t, 8),
        cost_estimate=pl.CostEstimate(
            flops=pixels * 72 * c * c, bytes_accessed=pixels * c * 16, transcendentals=pixels * c
        ),
    )(*held(args), *far(sources))
    return got if norm else [t, msg_in] + list(got)


def kernel_grad_kernel(with_prev, with_other, *refs):
    refs = list(refs)
    take = lambda n: [refs.pop(0) for _ in range(n)]
    info_ref, v_ref, edge_ref, norm_ref, small_ref, g_ref = take(6)
    prev_ref = take(1)[0] if with_prev else None
    other_ref = take(1)[0] if with_other else None
    out_ref = take(1)[0]
    send_ref = take(1)[0] if with_other else None
    a_ref, hi_ref, lo_ref, ghi_ref, glo_ref = refs
    cols, _, half, c = v_ref.shape
    rows = 2 * half
    mine = info_ref[2] == 1

    @pl.when(jnp.logical_not(mine))
    def _():
        out_ref[...] = prev_ref[...] if with_prev else jnp.zeros_like(out_ref)

    @pl.when(mine)
    def _():
        mean = norm_ref[0:1, :]
        gain = norm_ref[1:2, :] * small_ref[0:1, :]
        shift = small_ref[1:2, :]

        def act(x):
            u = (x - mean) * gain + shift
            return u * sigmoid(u)

        edge = act(edge_ref[0:rows, :].reshape(1, 2, half, c))
        put_edges(a_ref, info_ref[0], edge)

        def fill(at, n, carry):
            run = pl.ds(at, n)
            a_ref[pl.ds(1 + at, n)] = act(v_ref[run])
            return carry

        def tiles(at, n):
            put_tiles(hi_ref, lo_ref, a_ref, at, n)
            even, odd = [g_ref[pl.ds(at + t, n // 2, stride=2)] for t in range(2)]
            to = tiles_at(ghi_ref, at, n)
            for i, tile in enumerate((even, even + odd, even - odd, -odd)):
                for p in range(2):
                    hi, lo = split(tile[:, p])
                    ghi_ref[i, to, :, p * c : (p + 1) * c] = hi
                    glo_ref[i, to, :, p * c : (p + 1) * c] = lo

        def dot(a, b):
            return lax.dot_general(a, b, (((0,), (0,)), ((), ())), preferred_element_type=F32)

        n = 2 * hi_ref.shape[1]

        def products():
            m = []
            for i in range(4):
                hi, ghi = tile_of(hi_ref, i, 0, n), tile_of(ghi_ref, i, 0, n)
                acc = dot(hi, ghi) + dot(hi, tile_of(glo_ref, i, 0, n)) + dot(tile_of(lo_ref, i, 0, n), ghi)
                m.append([acc[a * c : (a + 1) * c, :c] + acc[(a + 1) * c : (a + 2) * c, c:] for a in range(3)])
            for a in range(3):
                both, apart = 0.5 * (m[1][a] + m[2][a]), 0.5 * (m[1][a] - m[2][a])
                for t, new in enumerate((m[0][a] + both, apart, both + m[3][a])):
                    to = slice((a * 3 + t) * c, (a * 3 + t + 1) * c)
                    out_ref[to, :] = out_ref[to, :] + new

        step = chunk_of(cols, 8)
        lax.fori_loop(0, cols // step, lambda j, _: fill(j * step, step, 0), 0)
        out_ref[...] = jnp.zeros_like(out_ref)

        def turn(j, _):
            tiles(j * n, n)
            products()
            return 0

        lax.fori_loop(0, cols // n, turn, 0)

    if with_other:
        keep_own = info_ref[0] == 0
        n = 9 * c // 16

        def exchange(j, _):
            at = pl.ds(pl.multiple_of(j * n, 8), n)
            own, other = out_ref[at, :], other_ref[at, :]
            out_ref[at, :] = jnp.where(keep_own, own, other)
            send_ref[at, :] = jnp.where(keep_own, other, own)
            return 0

        lax.fori_loop(0, 16, exchange, 0)


def kernel_grad(info, v, edge, norm, small, g, prev=None, other=None):
    cols, _, half, c = v.shape
    pixels = cols * half * 2
    args = [info, v, edge, norm, small, g] + [x for x in (prev, other) if x is not None]
    outs = [result((9 * c, c))] * (1 if other is None else 2)
    got = pl.pallas_call(
        functools.partial(kernel_grad_kernel, prev is not None, other is not None),
        out_shape=outs,
        in_specs=[SM] + [VM] * (len(args) - 1),
        out_specs=[VM] * len(outs),
        scratch_shapes=tile_scratch(cols, half, c)[:1]
        + [pltpu.VMEM((4, 256 // half, half, width * c), BF) for width in (4, 4, 2, 2)],
        compiler_params=room_for(v, 6),
        cost_estimate=pl.CostEstimate(
            flops=pixels * 72 * c * c, bytes_accessed=pixels * c * 8, transcendentals=pixels * c
        ),
    )(*held(args))
    return got[0] if other is None else got


def arrive_kernel(sources, info_ref, raw_ref, *refs):
    source_refs, (out_ref, msg_ref, after_ref, sem) = refs[:sources], refs[sources:]
    fetch(info_ref[1], 0, source_refs, after_ref, sem)
    rows, cols, c = raw_ref.shape
    one = two = jnp.zeros((8, c), F32)
    run = chunk_of(cols, RUN)
    for at in range(0, cols, run):
        for p in range(2):
            x = from_rows(raw_ref, at, run, p)
            out_ref[at : at + run, p] = x
            f = x.reshape(-1, 8, c)
            one = one + f.sum(0)
            two = two + (f * f).sum(0)
    last = jnp.where(info_ref[0] == 0, cols - 1, 0)
    msg_ref[0:rows, :] = out_ref[pl.ds(last, 1)].reshape(rows, c)
    msg_ref[rows : rows + 8, :] = pair_rows(one, two)
    fetched(0, source_refs, after_ref, sem)


def arrived(info, raw, sources):
    rows, cols, c = raw.shape
    return pl.pallas_call(
        functools.partial(arrive_kernel, len(sources)),
        out_shape=[result((cols, 2, rows // 2, c)), result((rows + 8, c)), result((3, 3, c, c))],
        in_specs=[SM, VM] + [HB] * len(sources),
        out_specs=[VM] * 3,
        scratch_shapes=[pltpu.SemaphoreType.DMA(())],
        compiler_params=room_for(raw, 4),
    )(info, raw, *far(sources))


def small_call(kernel, info, args, outs):
    total = sum(x.size for x in args) + sum(o.size for o in outs)
    return pl.pallas_call(
        kernel,
        out_shape=[result(o.shape) for o in outs],
        in_specs=[SM] * len(info) + [VM] * len(args),
        out_specs=[VM] * len(outs),
        compiler_params=pltpu.CompilerParams(vmem_limit_bytes=total * 8 + (2 << 20)),
    )(*info, *args)


def like(*shape):
    return jax.ShapeDtypeStruct(shape, F32)


def fold_kernel(by, info_ref, keep_ref, got_ref, out_ref, send_ref):
    n = out_ref.shape[0]
    upper = (info_ref[3] // by) % 2 == 1
    low = keep_ref[0:n, :] + got_ref[0:n, :]
    high = keep_ref[n:, :] + got_ref[n:, :]
    out_ref[...] = jnp.where(upper, high, low)
    send_ref[...] = jnp.where(upper, low, high)


def fold(info, by, keep, got):
    half = like(keep.shape[0] // 2, keep.shape[1])
    return small_call(functools.partial(fold_kernel, by), [info], [keep, got], [half, half])


def meet_kernel(info_ref, keep_ref, got_ref, out_ref, square_ref):
    out = keep_ref[...] + got_ref[...]
    out_ref[...] = out
    square_ref[...] = (out * out).reshape(-1, 8, out.shape[-1]).sum(0)


def meet(info, keep, got):
    return small_call(meet_kernel, [info], [keep, got], [keep, like(8, keep.shape[1])])


def unfold_kernel(by, info_ref, mine_ref, other_ref, out_ref):
    n = mine_ref.shape[0]
    upper = (info_ref[3] // by) % 2 == 1
    mine, other = mine_ref[...], other_ref[...]
    out_ref[0:n, :] = jnp.where(upper, other, mine)
    out_ref[n:, :] = jnp.where(upper, mine, other)


def unfold(info, by, mine, other):
    n, c = mine.shape
    return small_call(functools.partial(unfold_kernel, by), [info], [mine, other], [like(2 * n, c)])[0]


TABLE = 16


def spread_kernel(layers, rows, *refs):
    refs = list(refs)
    take = lambda n: [refs.pop(0) for _ in range(n)]
    infos = take(layers)
    parts_ref, square_ref, loss_ref = take(3)
    small = [0.0] * PAIR
    for l in range(layers):
        one_ref, bias1_ref, two_ref, bias2_ref = take(4)
        row = []
        for sums_ref, bias_ref in ((one_ref, bias1_ref), (two_ref, bias2_ref)):
            row += [sums_ref[rows + 1 : rows + 2, :], sums_ref[rows : rows + 1, :], bias_ref[0:1, :]]
        small[l % PAIR] += jnp.where(infos[l][2] == 1, jnp.concatenate(row, 0), 0.0)
    out_ref = take(1)[0]
    bands, n, c = parts_ref.shape
    share = parts_ref[...].sum(0)
    squares = square_ref[...].sum(0, keepdims=True) + (share * share).sum(0, keepdims=True)
    loss = loss_ref[rows : rows + 8, :].sum(0, keepdims=True)
    table = jnp.concatenate(small + [loss, squares, jnp.zeros((2, c), F32)], 0)
    for b in range(bands):
        out_ref[b, 0:n, :] = share
        out_ref[b, n : n + TABLE, :] = table


def spread(infos, rows, parts, square, loss, pieces):
    bands, n, c = parts.shape
    args = [parts, square, loss] + [x for piece in pieces for x in piece]
    kernel = functools.partial(spread_kernel, len(infos), rows)
    return small_call(kernel, infos, args, [like(bands, n + TABLE, c)])[0]


def table_kernel(info_ref, rest_ref, out_ref):
    out_ref[...] = rest_ref[:, rest_ref.shape[1] - TABLE :, :].sum(0)


def adam_step(w, first, second, grad, rate):
    first = 0.5 * first + 0.5 * grad
    second = 0.5 * second + 0.5 * grad * grad
    fix = 1.0 - 0.5**STEP
    step = first / fix / (jnp.sqrt(second / fix) + adam_eps) + decay_rate * w
    return w - rate * step, first, second


def tree_sum(items):
    while len(items) > 1:
        items = [a + b for a, b in zip(items[::2], items[1::2])]
    return items[0]


def adam_kernel(repeats, sections, *refs):
    refs = list(refs)
    take = lambda n: [refs.pop(0) for _ in range(n)]
    info_ref = take(1)[0]
    tables = [ref[...] for ref in take(sections)]
    rest_ref, got_rest_ref, odd_ref, got_odd_ref = take(4)
    small_refs = take(3)
    from_refs = take(3)
    new_small_refs = take(3)
    scalar_ref = take(1)[0]
    to_refs, old_refs, new_refs = take(3), take(3), take(3)
    in_sem, out_sem = refs
    bands = rest_ref.shape[0]
    n = from_refs[0].shape[1] // bands
    runs = [(which, run) for which in range(2) for run in range(bands)]

    def copies(sources, targets, sem, which, run):
        at = pl.ds(run * n, n)
        return [
            pltpu.make_async_copy(a.at[which, at], b.at[which, at], sem.at[k, which, run])
            for k, (a, b) in enumerate(zip(sources, targets))
        ]

    for which, run in runs:
        for copy in copies(from_refs, old_refs, in_sem, which, run):
            copy.start()
    chips = [tables[k] + tables[k + 1] for k in range(0, sections, PAIR)]
    squares = [jnp.sum(t[0:12] * t[0:12]) + jnp.sum(t[13:14]) for t in chips]
    norm = jnp.sqrt(jnp.full((8, 128), tree_sum(squares), F32))
    clip = clip_level / jnp.maximum(norm, clip_level)
    loss = jnp.full((8, 128), jnp.sum(chips[0][12:13]), F32) / repeats
    scalar_ref[0:8, :] = norm
    scalar_ref[8:16, :] = loss
    clip = clip[0:1, 0:1]
    first_core = info_ref[0] == 0
    grad = jnp.where(first_core, chips[0][0:6], chips[0][6:12]) * clip
    new = adam_step(*[ref[:, 0, :] for ref in small_refs], grad, rate_small)
    for ref, value in zip(new_small_refs, new):
        ref[:, 0, :] = value
    for which, run in runs:
        for copy in copies(from_refs, old_refs, in_sem, which, run):
            copy.wait()
        at = slice(run * n, (run + 1) * n)
        if which == 0:
            grad = jnp.where(first_core, rest_ref[run, 0:n, :], got_odd_ref[at, :])
        else:
            grad = jnp.where(first_core, got_rest_ref[run, 0:n, :], odd_ref[at, :])
        new = adam_step(*[ref[which, at, :] for ref in old_refs], grad * clip, rate_conv)
        for ref, value in zip(new_refs, new):
            ref[which, at, :] = value
        for copy in copies(new_refs, to_refs, out_sem, which, run):
            copy.start()
    for which, run in runs:
        for copy in copies(new_refs, to_refs, out_sem, which, run):
            copy.wait()


def optimizer(info, repeats, tables, rest, got_rest, odd, got_odd, smalls, states):
    shape, bands = states[0].shape, rest.shape[0]
    args = [*tables, rest, got_rest, odd, got_odd, *smalls]
    sems = pltpu.SemaphoreType.DMA((3, 2, bands))
    return pl.pallas_call(
        functools.partial(adam_kernel, repeats, len(tables)),
        out_shape=[like(*x.shape) for x in smalls] + [like(16, 128)] + [pltpu.HBM(shape, F32)] * 3,
        in_specs=[SM] + [VM] * len(args) + [HB] * 3,
        out_specs=[VM] * 4 + [HB] * 3,
        scratch_shapes=[pltpu.VMEM(shape, F32)] * 6 + [sems] * 2,
        compiler_params=pltpu.CompilerParams(vmem_limit_bytes=11 * states[0].size * 4),
    )(info, *args, *far(states))


def partner(x):
    return lax.ppermute(x, "section", [(i, i ^ 1) for i in range(lax.axis_size("section"))])


def to_image(bands, repeats):
    bands = jnp.repeat(bands, repeats, 0) if repeats > 1 else bands
    got = lax.all_to_all(bands, "band", 0, 0, tiled=True)
    return got.reshape(-1, *got.shape[2:])


def crossed(x, by):
    return lax.ppermute(x, "band", [(i, i ^ by) for i in range(lax.axis_size("band"))])


def band_bits():
    return [1 << k for k in range(lax.axis_size("band").bit_length() - 1)]


def swapped(parts):
    return lax.all_to_all(parts, "band", 0, 0, tiled=True)


def local(
    images,
    targets,
    masks,
    conv_weights,
    small_params,
    conv_first,
    conv_second,
    small_first,
    small_second,
):
    sections = lax.axis_size("section")
    bands = lax.axis_size("band")
    here = lax.axis_index("section")
    core = here % PAIR
    chip = here // PAIR
    chips = sections // PAIR
    layers = sections
    micro, part, width, c = images.shape
    repeats = bands // micro
    cols = width // PAIR
    rows = part * bands
    half = rows // 2

    image = to_image(lax.dynamic_slice_in_dim(images, core * cols, cols, 2), repeats)
    lengths = jnp.sum(masks.astype(F32), 2)
    counts = jnp.where(jnp.arange(part)[None, :] == 0, jnp.sum(lengths), 0.0)
    extra = jnp.stack([lengths, jnp.broadcast_to(counts, lengths.shape)] + [jnp.zeros_like(lengths)] * 6, 2)
    extra = jnp.broadcast_to(extra[..., None], (micro, part, 8, c))
    target = jnp.concatenate([lax.dynamic_slice_in_dim(targets, core * cols, cols, 2), extra], 2)
    image, target = lax.optimization_barrier((image, target))
    target = to_image(target, repeats)

    own = (conv_weights[0], jnp.pad(small_params[0], ((0, 2), (0, 0))))
    sources, smalls = [], []
    for k in range(chips):
        shift = [((i + PAIR * k) % sections, i) for i in range(sections)]
        theirs = own if k == 0 else tuple(lax.ppermute(x, "section", shift) for x in own)
        others = tuple(partner(x) for x in theirs)
        sources += [theirs[0], others[0]]
        smalls += [theirs[1], others[1]]
    smalls = jnp.stack(smalls)

    def pick_of(layer):
        return PAIR * ((layer // PAIR - chip) % chips) + (layer % PAIR != core).astype(jnp.int32)

    def info_of(layer):
        mine = (chip == layer // PAIR).astype(jnp.int32)
        active = (chip <= layer // PAIR).astype(jnp.int32)
        info = [core, pick_of(layer), mine, lax.axis_index("band"), active]
        return jnp.stack(info).astype(jnp.int32)

    def norms_of(layer):
        both = lax.dynamic_index_in_dim(smalls, pick_of(layer), 0, False)
        return jnp.pad(both[0:3], ((0, 5), (0, 0))), jnp.pad(both[3:6], ((0, 5), (0, 0)))

    infos = [info_of(l) for l in range(layers)]
    norms = [norms_of(l) for l in range(layers)]
    image, infos, norms = lax.optimization_barrier((image, infos, norms))
    again_first = not is_near(jax.ShapeDtypeStruct((cols, rows, c), F32))
    order = [(l, k) for l in range(layers) for k in range(2)]
    for l in reversed(range(layers)):
        order += [(l, 0)] * again_first + [(l, 1), (l, 0)]
    order = [(infos[l], k) for l, k in order[1:]] + [(infos[0], 0)]

    def with_next(w):
        return w, sources, order.pop(0)

    field, message, w = arrived(infos[0], image, sources)
    stack = []
    for l in range(layers):
        got = partner(message)
        mid, sent, norm, w = conv_forward(infos[l], with_next(w), field, got, message, norms[l][0])
        again = partner(sent)
        one, first_in = (field, got, norm), (field, got, message, norms[l][0])
        goal = (target, repeats) if l == layers - 1 else ()
        field, message, norm, w, *count = conv_forward(
            infos[l], with_next(w), mid, again, sent, norms[l][1], field, *goal
        )
        stack.append((one, (None if again_first else mid, again, norm), first_in))

    def second_back(l, w, t, got, enter, res):
        _, (v2, e2, n2), first_in = stack[l]
        if again_first:
            t, first_in = lax.optimization_barrier((t, first_in))
            v2, _, _, w = conv_forward(infos[l], with_next(w), *first_in)
        grad, grad_edge, t, sent, bias, w = conv_backward(
            infos[l], with_next(w), t, got, v2, n2, norms[l][1], norm=enter, res=res
        )
        return w, t, partner(sent), bias, (sent, v2, e2, n2, norms[l][1]), (grad, grad_edge)

    def grad_of(l, k, v, g, prev, other=None):
        _, edge, norm = stack[l][k]
        return kernel_grad(infos[l], v, edge, norm, norms[l][k], g, prev, other)

    grad, (count,) = field, count
    got = partner(message)
    loss_message = message

    t, enter, res = grad, None, None
    slots = [[None, None] for _ in range(PAIR)]
    pieces = {}
    for l in reversed(range(1, layers)):
        slot = slots[l % PAIR]
        w, t, got, bias2, enter, res = second_back(l, w, t, got, enter, res)
        k2 = grad_of(l, 1, enter[1], res[0], slot[1])
        sent = enter[0]
        v1, e1, n1 = stack[l][0]
        mid, _, t, message, bias1, w = conv_backward(
            infos[l], with_next(w), t, got, v1, n1, norms[l][0], norm=enter
        )
        got = partner(message)
        k1 = grad_of(l, 0, v1, mid, slot[0], k2 if l == 1 else None)
        enter = (message, v1, e1, n1, norms[l][0])
        slot[:] = [k1, k2]
        pieces[l] = (message, bias1, sent, bias2)

    keep, send = slots[1][0]
    info, bits = infos[0], band_bits()
    keep, send = fold(info, bits[0], keep, partner(send))
    got_odd = crossed(send, bits[0])
    w, t, got, bias2, enter, res = second_back(0, w, t, got, enter, res)
    mid, got_odd = lax.optimization_barrier((res[0], got_odd))
    keep, send = fold(info, bits[1], keep, got_odd)
    got_odd = crossed(send, bits[1])
    k2 = grad_of(0, 1, enter[1], mid, slots[0][1])
    t, k2, got_odd = lax.optimization_barrier((t, k2, got_odd))
    for by in bits[2:-1]:
        keep, send = fold(info, by, keep, got_odd)
        got_odd = crossed(send, by)
    keep, send = fold(info, bits[-1], keep, got_odd)
    mid, mid_edge, bias1 = norm_enter(t, got, enter)
    mid, send = lax.optimization_barrier((mid, send))
    got_odd = crossed(send, bits[-1])
    sent = enter[0]
    v1, e1, n1 = stack[0][0]
    even, send = grad_of(0, 0, v1, mid, slots[0][0], k2)
    even, send, got_odd = lax.optimization_barrier((even, send, got_odd))
    send = partner(send)
    odd, odd_square = meet(info, keep, got_odd)
    even, odd = lax.optimization_barrier((even, odd))
    odd_got = crossed(odd, bits[-1])
    even = meet(info, even, send)[0]
    even, odd_got = lax.optimization_barrier((even, odd_got))
    odd = unfold(info, bits[-1], odd, odd_got)
    mid, even, odd = lax.optimization_barrier((mid, even, odd))
    odd_got = crossed(odd, bits[-2])
    parts = swapped(even.reshape(bands, -1, c))
    _, _, _, message, _, _ = conv_backward(
        info, with_next(w), mid, mid_edge, v1, n1, norms[0][0]
    )
    pieces[0] = (message, bias1, sent, bias2)
    message, odd_got = lax.optimization_barrier((message, odd_got))
    odd = unfold(info, bits[-2], odd, odd_got)
    for by in bits[-3::-1]:
        odd = unfold(info, by, odd, crossed(odd, by))
    got_odd = partner(odd)
    rest = spread(infos, rows, parts, odd_square, loss_message, [pieces[l] for l in range(layers)])
    rest = swapped(rest)
    table = small_call(table_kernel, [info], [rest], [like(TABLE, c)])[0]
    got_rest = partner(rest)
    tables = [table]
    for by in range(1, sections):
        tables.append(lax.ppermute(table, "section", [(i, i ^ by) for i in range(sections)]))

    flat = lambda x: x.reshape(2, 9 * c, c)
    smalls = [x.transpose(1, 0, 2) for x in (small_params, small_first, small_second)]
    states = [flat(x) for x in (conv_weights, conv_first, conv_second)]
    *new_smalls, scalars, new_conv, new_conv_first, new_conv_second = optimizer(
        info, repeats, tables, rest, got_rest, odd, got_odd, smalls, states
    )
    new_conv, new_conv_first, new_conv_second = [
        x.reshape(conv_weights.shape) for x in (new_conv, new_conv_first, new_conv_second)
    ]
    new_small, new_small_first, new_small_second = [x.transpose(1, 0, 2) for x in new_smalls]
    grad_norm, loss_sum, valid_count = scalars[0, 0], scalars[8, 0], count[0, 0]
    return (
        new_conv,
        new_conv_first,
        new_conv_second,
        new_small,
        new_small_first,
        new_small_second,
        loss_sum,
        valid_count,
        grad_norm,
    )


def solution(mesh):
    in_specs = (
        P(None, "band", None, None),
        P(None, "band", None, None),
        P(None, "band", None),
        P("section", None, None, None, None, None),
        P("section", None, None),
        P("section", None, None, None, None, None),
        P("section", None, None, None, None, None),
        P("section", None, None),
        P("section", None, None),
    )
    out_specs = (
        P("section", None, None, None, None, None),
        P("section", None, None, None, None, None),
        P("section", None, None, None, None, None),
        P("section", None, None),
        P("section", None, None),
        P("section", None, None),
        P(),
        P(),
        P(),
    )
    return jax.shard_map(local, mesh=mesh, in_specs=in_specs, out_specs=out_specs, check_vma=False)
```

```python
import functools

import jax
import jax.numpy as jnp
from jax import lax
from jax.experimental import pallas as pl
from jax.experimental.pallas import tpu as pltpu
from jax.sharding import PartitionSpec as P

GROUPS = 32
STEP = 10
PAIR = 2

clip_level = 0.01
rate_conv = 0.02
rate_small = 0.2
adam_eps = 1e-08
decay_rate = 0.01

BF = jnp.bfloat16
F32 = jnp.float32
VM = pl.BlockSpec(memory_space=pltpu.VMEM)
SM = pl.BlockSpec(memory_space=pltpu.SMEM)
HB = pl.BlockSpec(memory_space=pltpu.HBM)


def split(x):
    hi = x.astype(BF)
    return hi, (x - hi.astype(F32)).astype(BF)


def group_sum(row, per):
    lane = lax.broadcasted_iota(jnp.int32, row.shape, 1)
    width = row.shape[1]
    step = 1
    while step < per:
        other = jnp.where(
            (lane // step) % 2 == 0, pltpu.roll(row, width - step, 1), pltpu.roll(row, step, 1)
        )
        row = row + other
        step *= 2
    return row


def sigmoid(u):
    return 0.5 * jnp.tanh(0.5 * u) + 0.5


def tiles_at(ref, at, n):
    return pl.ds(0 if ref.shape[1] == n // 2 else at // 2, n // 2)


def put_tiles(hi_ref, lo_ref, a_ref, at, n):
    _, _, half, c = a_ref.shape
    d = [a_ref[pl.ds(at + t, n // 2, stride=2)] for t in range(4)]
    k = lax.broadcasted_iota(jnp.int32, (n // 2, half, c), 1)
    to = tiles_at(hi_ref, at, n)
    for i, tile in enumerate((d[0] - d[2], d[1] + d[2], d[2] - d[1], d[1] - d[3])):
        even, odd = tile[:, 0], tile[:, 1]
        down = jnp.where(k == 0, 0.0, pltpu.roll(odd, 1, 1))
        up = jnp.where(k == half - 1, 0.0, pltpu.roll(even, half - 1, 1))
        for q, part in enumerate((down, even, odd, up)):
            hi, lo = split(part)
            hi_ref[i, to, :, q * c : (q + 1) * c] = hi
            lo_ref[i, to, :, q * c : (q + 1) * c] = lo


def put_edges(a_ref, side, edge):
    cols = a_ref.shape[0] - 2
    a_ref[0:1] = jnp.where(side == 1, edge, 0.0)
    a_ref[cols + 1 : cols + 2] = jnp.where(side == 0, edge, 0.0)


def tile_of(ref, i, at, n):
    _, _, half, width = ref.shape
    return ref[i, tiles_at(ref, at, n)].reshape(n // 2 * half, width)


def pair_products(hi_ref, lo_ref, whi_ref, wlo_ref, at, n, dot):
    m = []
    for i in range(4):
        hi = tile_of(hi_ref, i, at, n)
        w = whi_ref[i]
        m.append(dot(hi, w) + dot(hi, wlo_ref[i]) + dot(tile_of(lo_ref, i, at, n), w))
    return m[0] + (m[1] + m[2]), (m[1] - m[2]) - m[3]


def pair_rows(one, two):
    return jnp.concatenate(
        [one.sum(0, keepdims=True), two.sum(0, keepdims=True), jnp.zeros((6, one.shape[1]), F32)], 0
    )


def chunk_of(cols, most):
    return max(n for n in range(1, most + 1) if cols % n == 0)


NEAR = 2 << 20


def is_near(x):
    return x.size * 4 <= NEAR


def room_for(field, fields):
    room = 5 if is_near(field) else fields + 1
    return pltpu.CompilerParams(vmem_limit_bytes=room * field.size * 4 + (6 << 20))


def result(shape):
    near = pltpu.VMEM(shape, F32)
    return near if is_near(jax.ShapeDtypeStruct(shape, F32)) else jax.ShapeDtypeStruct(shape, F32)


def held(args):
    return [
        pltpu.with_memory_space_constraint(x, pltpu.VMEM) if x.ndim == 4 and is_near(x) else x
        for x in args
    ]


def far(args):
    return [pltpu.with_memory_space_constraint(x, pltpu.HBM) for x in args]


def fetch(pick, which, sources, into, sem):
    for k, source in enumerate(sources):

        @pl.when(pick == k)
        def _(source=source):
            pltpu.make_async_copy(source.at[which], into, sem).start()


def fetched(which, sources, into, sem):
    pltpu.make_async_copy(sources[0].at[which], into, sem).wait()


def pack(w_ref, hi_ref, lo_ref, flipped):
    c = w_ref.shape[-1]
    zero = jnp.zeros((c, c), BF)
    for a in range(3):
        if flipped:
            g0, g1, g2 = [w_ref[2 - a, 2 - t] for t in range(3)]
        else:
            g0, g1, g2 = [w_ref[a, t] for t in range(3)]
        both, mid = 0.5 * (g0 + g2), 0.5 * g1
        for i, g in enumerate((g0, both + mid, both - mid, g2)):
            hi, lo = split(g)
            for p in range(2):
                q, p = slice((a + p) * c, (a + p + 1) * c), slice(p * c, (p + 1) * c)
                at = (i, p, q) if flipped else (i, q, p)
                hi_ref[at], lo_ref[at] = hi, lo
    for i in range(4):
        for q, p in ((0, 1), (3, 0)):
            q, p = slice(q * c, (q + 1) * c), slice(p * c, (p + 1) * c)
            at = (i, p, q) if flipped else (i, q, p)
            hi_ref[at], lo_ref[at] = zero, zero


RUN = 32
FAR_RUN = 4


def in_turns(unrolled, cols, fill, tiles, ready, conv, carry):
    if not unrolled:
        n = FAR_RUN
        runs = cols // n
        carry = lax.fori_loop(0, runs, lambda j, c: fill(j * n, n, c), carry)
        ready()

        def step(j, carry):
            tiles(j * n, n)
            return conv(j * n, n, carry)

        return lax.fori_loop(0, runs, step, carry)
    n = chunk_of(cols, RUN)
    done = min(cols, n + 2)
    carry = fill(0, done, carry)
    tiles(0, n)
    ready()
    for at in range(0, cols, n):
        carry = conv(at, n, carry)
        more = min(n, cols - done)
        if more > 0:
            carry = fill(done, more, carry)
            done += more
        if at + n < cols:
            tiles(at + n, n)
    return carry


def from_rows(ref, at, n, p):
    half = ref.shape[0] // 2
    return jnp.swapaxes(ref[pl.ds(p, half, stride=2), pl.ds(at, n), :], 0, 1)


def target_of(ref, at, n, p):
    if isinstance(at, int):
        x = from_rows(ref, at, n, p)
    else:
        wide = from_rows(ref, pl.multiple_of(at // 8 * 8, 8), 8, p)
        x = jnp.where(at % 8 == 0, wide[:n], wide[8 - n :])
    x = x.reshape(n // 2, 2, *x.shape[1:])
    return x[:, 0], x[:, 1]


def forward_kernel(sources, following, with_res, repeats, *refs):
    refs = list(refs)
    take = lambda n: [refs.pop(0) for _ in range(n)]
    info_ref, next_ref, w_ref, v_ref, in_ref, own_ref, small_ref = take(7)
    res_ref = take(1)[0] if with_res else None
    goal_ref = take(1)[0] if repeats else None
    source_refs = take(sources)
    if repeats:
        count_ref = refs.pop(4)
        raw_ref, raw_sem = refs.pop(), refs.pop()
        goal = pltpu.make_async_copy(goal_ref, raw_ref, raw_sem)
        goal.start()
    out_ref, msg_ref, norm_ref, after_ref, a_ref, hi_ref, lo_ref, whi_ref, wlo_ref, sem = refs
    cols, _, half, c = v_ref.shape
    rows = 2 * half
    side = info_ref[0]
    fetch(next_ref[1], following, source_refs, after_ref, sem)
    per = c // GROUPS
    count = float(PAIR * cols * rows * per)
    sums = group_sum(own_ref[rows : rows + 8, :] + in_ref[rows : rows + 8, :], per) / count
    mean = sums[0:1]
    inv = lax.rsqrt(sums[1:2] - mean * mean + 1e-05)
    norm_ref[0:1, :] = mean
    norm_ref[1:2, :] = inv
    norm_ref[2:8, :] = jnp.zeros((6, c), F32)
    gain = inv * small_ref[0:1, :]
    shift = small_ref[1:2, :]
    bias = small_ref[2:3, :]

    def act(x):
        u = (x - mean) * gain + shift
        return u * sigmoid(u)

    put_edges(a_ref, side, act(in_ref[0:rows, :].reshape(1, 2, half, c)))

    lengths = []

    def ready():
        pack(w_ref, whi_ref, wlo_ref, False)
        if repeats:
            goal.wait()
            count = jnp.zeros((1, c), F32)
            for p in range(2):
                extra = from_rows(raw_ref, cols, 8, p)
                lengths.append(extra[0])
                count = count + extra[1].sum(0, keepdims=True)
            count_ref[...] = jnp.broadcast_to(count, (8, c))

    def fill(at, n, carry):
        a_ref[pl.ds(1 + at, n)] = act(v_ref[pl.ds(at, n)])
        return carry

    def tiles(at, n):
        put_tiles(hi_ref, lo_ref, a_ref, at, n)

    def dot(a, b):
        return jnp.dot(a, b, preferred_element_type=F32)

    def conv(at, n, carry):
        one, two = carry
        if repeats:
            scale = 1.0 / (count_ref[0:1, :] * repeats)
            target = [target_of(raw_ref, at, n, p) for p in range(2)]
        for t, acc in enumerate(pair_products(hi_ref, lo_ref, whi_ref, wlo_ref, at, n, dot)):
            to = pl.ds(at + t, n // 2, stride=2)
            for p in range(2):
                o = (acc[:, p * c : (p + 1) * c] + bias).reshape(n // 2, half, c)
                if with_res:
                    o = o + res_ref[to, p]
                if repeats:
                    pair = lax.broadcasted_iota(jnp.int32, o.shape, 0)
                    valid = (side * cols + at + t + 2 * pair).astype(F32) < lengths[p][None]
                    diff = o - target[p][t]
                    square = diff * diff + 1.0
                    out_ref[to, p] = jnp.where(valid, diff * lax.rsqrt(square) * scale, 0.0)
                    part = jnp.where(valid, jnp.sqrt(square) - 1.0, 0.0)
                    one = one + part.reshape(-1, 8, c).sum(0)
                    continue
                out_ref[to, p] = o
                f = o.reshape(-1, 8, c)
                one = one + f.sum(0)
                two = two + (f * f).sum(0)
        return one, two

    zero = jnp.zeros((8, c), F32)
    one, two = in_turns(is_near(v_ref), cols, fill, tiles, ready, conv, (zero, zero))
    last = jnp.where(side == 0, cols - 1, 0)
    msg_ref[0:rows, :] = out_ref[pl.ds(last, 1)].reshape(rows, c)
    msg_ref[rows : rows + 8, :] = pair_rows(one, two)
    fetched(following, source_refs, after_ref, sem)


def tile_scratch(cols, half, c, lanes=(4, 4)):
    field = (cols, 2, half, c)
    pairs = (cols if is_near(jax.ShapeDtypeStruct(field, F32)) else FAR_RUN) // 2
    tiles = [pltpu.VMEM((4, pairs, half, width * c), BF) for width in lanes]
    return [pltpu.VMEM((cols + 2, 2, half, c), F32)] + tiles


def conv_scratch(cols, half, c, packed):
    return (
        tile_scratch(cols, half, c) + [pltpu.VMEM(packed, BF)] * 2 + [pltpu.SemaphoreType.DMA(())]
    )


def conv_forward(info, weights, v, msg_in, msg_own, small, res=None, raw=None, repeats=0):
    cols, _, half, c = v.shape
    rows = 2 * half
    w, sources, (info_next, following) = weights
    args = [info, info_next, w, v, msg_in, msg_own, small] + ([] if res is None else [res])
    distant = ([] if raw is None else [raw]) + sources
    goal = [] if raw is None else [pltpu.SemaphoreType.DMA(()), pltpu.VMEM(raw.shape, F32)]
    pixels = cols * rows
    return pl.pallas_call(
        functools.partial(forward_kernel, len(sources), following, res is not None, repeats),
        out_shape=[result(v.shape), result((rows + 8, c)), result((8, c)), result(w.shape)]
        + [result((8, c))] * bool(repeats),
        in_specs=[SM, SM] + [VM] * (len(args) - 2) + [HB] * len(distant),
        out_specs=[VM] * (5 if repeats else 4),
        scratch_shapes=conv_scratch(cols, half, c, (4, 4 * c, 2 * c)) + goal,
        compiler_params=room_for(v, 7 if repeats else 6),
        cost_estimate=pl.CostEstimate(
            flops=pixels * 72 * c * c, bytes_accessed=pixels * c * 8, transcendentals=pixels * c
        ),
    )(*held(args), *far(distant))


def enter_norm(own_ref, in_ref, norm_ref, small_ref, cols, rows):
    c = own_ref.shape[-1]
    per = c // GROUPS
    count = float(PAIR * cols * rows * per)
    gain = small_ref[0:1, :]
    mean = norm_ref[0:1, :]
    inv = norm_ref[1:2, :]
    sums = own_ref[rows : rows + 8, :] + in_ref[rows : rows + 8, :]
    means = group_sum(sums * gain, per) / count
    first, second = means[0:1], means[1:2]

    def enter(t, v):
        return inv * (t * gain - first - (v - mean) * inv * second)

    return enter


def enter_kernel(t_ref, in_ref, own_ref, v_ref, edge_ref, norm_ref, small_ref, g_ref, ge_ref, bias_ref):
    cols, _, half, c = t_ref.shape
    rows = 2 * half
    enter = enter_norm(own_ref, in_ref, norm_ref, small_ref, cols, rows)
    edge = enter(in_ref[0:rows, :], edge_ref[0:rows, :])
    ge_ref[0:rows, :] = edge
    ge_ref[rows : rows + 8, :] = jnp.zeros((8, c), F32)
    n = chunk_of(cols, 8)

    def fill(j, total):
        at = pl.ds(j * n, n)
        g = enter(t_ref[at], v_ref[at])
        g_ref[at] = g
        return total + g.reshape(-1, 8, c).sum(0)

    total = lax.fori_loop(0, cols // n, fill, jnp.zeros((8, c), F32))
    bias_ref[...] = jnp.broadcast_to(total.sum(0, keepdims=True), (8, c))


def norm_enter(t, msg_in, norm):
    cols, _, half, c = t.shape
    return pl.pallas_call(
        enter_kernel,
        out_shape=[
            result(t.shape),
            result((2 * half + 8, c)),
            result((8, c)),
        ],
        in_specs=[VM] * 7,
        out_specs=[VM] * 3,
        compiler_params=room_for(t, 4),
    )(*held([t, msg_in, *norm]))


def backward_kernel(sources, following, with_norm, with_res, info_ref, *refs):
    @pl.when(info_ref[4] == 1)
    def _():
        backward_body(sources, following, with_norm, with_res, info_ref, *refs)


def backward_body(sources, following, with_norm, with_res, *refs):
    refs = list(refs)
    take = lambda n: [refs.pop(0) for _ in range(n)]
    info_ref, next_ref, w_ref, t_ref, in_ref = take(5)
    if with_norm:
        own_ref, vp_ref, vpe_ref, normp_ref, smallp_ref = take(5)
    if with_res:
        res_ref, rese_ref = take(2)
    ve_ref, norme_ref, smalle_ref = take(3)
    source_refs = take(sources)
    if with_norm:
        g_ref, ge_ref = take(2)
    out_ref, msg_ref, bias_ref, after_ref, a_ref, hi_ref, lo_ref, bhi_ref, blo_ref, sem = refs
    cols, _, half, c = t_ref.shape
    rows = 2 * half
    side = info_ref[0]
    fetch(next_ref[1], following, source_refs, after_ref, sem)
    edge = in_ref[0:rows, :]
    if with_norm:
        enter = enter_norm(own_ref, in_ref, normp_ref, smallp_ref, cols, rows)
        edge = enter(edge, vpe_ref[0:rows, :])
        if with_res:
            edge = edge + rese_ref[0:rows, :]
        ge_ref[0:rows, :] = edge
        ge_ref[rows : rows + 8, :] = jnp.zeros((8, c), F32)
    put_edges(a_ref, side, edge.reshape(1, 2, half, c))
    zero = jnp.zeros((8, c), F32)

    def ready():
        pack(w_ref, bhi_ref, blo_ref, True)

    def fill(at, n, carry):
        one, two, total = carry
        run = pl.ds(at, n)
        g = t_ref[run]
        if with_norm:
            g = enter(g, vp_ref[run])
            if with_res:
                g = g + res_ref[run]
            g_ref[run] = g
        a_ref[pl.ds(1 + at, n)] = g
        return one, two, total + g.reshape(-1, 8, c).sum(0)

    gain_e, shift_e = smalle_ref[0:1, :], smalle_ref[1:2, :]
    mean_e, inv_e = norme_ref[0:1, :], norme_ref[1:2, :]

    def dot(a, b):
        return lax.dot_general(a, b, (((1,), (1,)), ((), ())), preferred_element_type=F32)

    def conv(at, n, carry):
        one, two, total = carry
        for k, acc in enumerate(pair_products(hi_ref, lo_ref, bhi_ref, blo_ref, at, n, dot)):
            to = pl.ds(at + k, n // 2, stride=2)
            for p in range(2):
                q = acc[:, p * c : (p + 1) * c].reshape(n // 2, half, c)
                normed = (ve_ref[to, p] - mean_e) * inv_e
                u = normed * gain_e + shift_e
                s = sigmoid(u)
                t = q * (s * (1.0 + u * (1.0 - s)))
                out_ref[to, p] = t
                one = one + t.reshape(-1, 8, c).sum(0)
                two = two + (t * normed).reshape(-1, 8, c).sum(0)
        return one, two, total

    def tiles(at, n):
        put_tiles(hi_ref, lo_ref, a_ref, at, n)

    one, two, total = in_turns(is_near(t_ref), cols, fill, tiles, ready, conv, (zero, zero, zero))
    bias_ref[...] = jnp.broadcast_to(total.sum(0, keepdims=True), (8, c))
    last = jnp.where(side == 0, cols - 1, 0)
    msg_ref[0:rows, :] = out_ref[pl.ds(last, 1)].reshape(rows, c)
    msg_ref[rows : rows + 8, :] = pair_rows(one, two)
    fetched(following, source_refs, after_ref, sem)


def conv_backward(info, weights, t, msg_in, v_e, norm_e, small_e, norm=None, res=None):
    cols, _, half, c = t.shape
    rows = 2 * half
    w, sources, (info_next, following) = weights
    args = [info, info_next, w, t, msg_in] + list(norm or ()) + list(res or ())
    args += [v_e, norm_e, small_e]
    field, msg = result(t.shape), result((rows + 8, c))
    outs = ([field, msg] if norm else []) + [field, msg, result((8, c)), result(w.shape)]
    pixels = cols * rows
    places = {}
    if norm and not is_near(t):
        places = {3: 2, 10: 0} if res else {3: 2}
    got = pl.pallas_call(
        functools.partial(backward_kernel, len(sources), following, norm is not None, res is not None),
        out_shape=outs,
        input_output_aliases=places,
        in_specs=[SM, SM] + [VM] * (len(args) - 2) + [HB] * len(sources),
        out_specs=[VM] * len(outs),
        scratch_shapes=conv_scratch(cols, half, c, (4, 2 * c, 4 * c)),
        compiler_params=room_for(t, 8),
        cost_estimate=pl.CostEstimate(
            flops=pixels * 72 * c * c, bytes_accessed=pixels * c * 16, transcendentals=pixels * c
        ),
    )(*held(args), *far(sources))
    return got if norm else [t, msg_in] + list(got)


def kernel_grad_kernel(with_prev, with_other, *refs):
    refs = list(refs)
    take = lambda n: [refs.pop(0) for _ in range(n)]
    info_ref, v_ref, edge_ref, norm_ref, small_ref, g_ref = take(6)
    prev_ref = take(1)[0] if with_prev else None
    other_ref = take(1)[0] if with_other else None
    out_ref = take(1)[0]
    send_ref = take(1)[0] if with_other else None
    a_ref, hi_ref, lo_ref, ghi_ref, glo_ref = refs
    cols, _, half, c = v_ref.shape
    rows = 2 * half
    mine = info_ref[2] == 1

    @pl.when(jnp.logical_not(mine))
    def _():
        out_ref[...] = prev_ref[...] if with_prev else jnp.zeros_like(out_ref)

    @pl.when(mine)
    def _():
        mean = norm_ref[0:1, :]
        gain = norm_ref[1:2, :] * small_ref[0:1, :]
        shift = small_ref[1:2, :]

        def act(x):
            u = (x - mean) * gain + shift
            return u * sigmoid(u)

        edge = act(edge_ref[0:rows, :].reshape(1, 2, half, c))
        put_edges(a_ref, info_ref[0], edge)

        def fill(at, n, carry):
            run = pl.ds(at, n)
            a_ref[pl.ds(1 + at, n)] = act(v_ref[run])
            return carry

        def tiles(at, n):
            put_tiles(hi_ref, lo_ref, a_ref, at, n)
            even, odd = [g_ref[pl.ds(at + t, n // 2, stride=2)] for t in range(2)]
            to = tiles_at(ghi_ref, at, n)
            for i, tile in enumerate((even, even + odd, even - odd, -odd)):
                for p in range(2):
                    hi, lo = split(tile[:, p])
                    ghi_ref[i, to, :, p * c : (p + 1) * c] = hi
                    glo_ref[i, to, :, p * c : (p + 1) * c] = lo

        def dot(a, b):
            return lax.dot_general(a, b, (((0,), (0,)), ((), ())), preferred_element_type=F32)

        n = 2 * hi_ref.shape[1]

        def products():
            m = []
            for i in range(4):
                hi, ghi = tile_of(hi_ref, i, 0, n), tile_of(ghi_ref, i, 0, n)
                acc = dot(hi, ghi) + dot(hi, tile_of(glo_ref, i, 0, n)) + dot(tile_of(lo_ref, i, 0, n), ghi)
                m.append([acc[a * c : (a + 1) * c, :c] + acc[(a + 1) * c : (a + 2) * c, c:] for a in range(3)])
            for a in range(3):
                both, apart = 0.5 * (m[1][a] + m[2][a]), 0.5 * (m[1][a] - m[2][a])
                for t, new in enumerate((m[0][a] + both, apart, both + m[3][a])):
                    to = slice((a * 3 + t) * c, (a * 3 + t + 1) * c)
                    out_ref[to, :] = out_ref[to, :] + new

        step = chunk_of(cols, 8)
        lax.fori_loop(0, cols // step, lambda j, _: fill(j * step, step, 0), 0)
        out_ref[...] = jnp.zeros_like(out_ref)

        def turn(j, _):
            tiles(j * n, n)
            products()
            return 0

        lax.fori_loop(0, cols // n, turn, 0)

    if with_other:
        keep_own = info_ref[0] == 0
        n = 9 * c // 16

        def exchange(j, _):
            at = pl.ds(pl.multiple_of(j * n, 8), n)
            own, other = out_ref[at, :], other_ref[at, :]
            out_ref[at, :] = jnp.where(keep_own, own, other)
            send_ref[at, :] = jnp.where(keep_own, other, own)
            return 0

        lax.fori_loop(0, 16, exchange, 0)


def kernel_grad(info, v, edge, norm, small, g, prev=None, other=None):
    cols, _, half, c = v.shape
    pixels = cols * half * 2
    args = [info, v, edge, norm, small, g] + [x for x in (prev, other) if x is not None]
    outs = [result((9 * c, c))] * (1 if other is None else 2)
    got = pl.pallas_call(
        functools.partial(kernel_grad_kernel, prev is not None, other is not None),
        out_shape=outs,
        in_specs=[SM] + [VM] * (len(args) - 1),
        out_specs=[VM] * len(outs),
        scratch_shapes=tile_scratch(cols, half, c)[:1]
        + [pltpu.VMEM((4, 256 // half, half, width * c), BF) for width in (4, 4, 2, 2)],
        compiler_params=room_for(v, 6),
        cost_estimate=pl.CostEstimate(
            flops=pixels * 72 * c * c, bytes_accessed=pixels * c * 8, transcendentals=pixels * c
        ),
    )(*held(args))
    return got[0] if other is None else got


def arrive_kernel(sources, info_ref, raw_ref, *refs):
    source_refs, (out_ref, msg_ref, after_ref, sem) = refs[:sources], refs[sources:]
    fetch(info_ref[1], 0, source_refs, after_ref, sem)
    rows, cols, c = raw_ref.shape
    one = two = jnp.zeros((8, c), F32)
    run = chunk_of(cols, RUN)
    for at in range(0, cols, run):
        for p in range(2):
            x = from_rows(raw_ref, at, run, p)
            out_ref[at : at + run, p] = x
            f = x.reshape(-1, 8, c)
            one = one + f.sum(0)
            two = two + (f * f).sum(0)
    last = jnp.where(info_ref[0] == 0, cols - 1, 0)
    msg_ref[0:rows, :] = out_ref[pl.ds(last, 1)].reshape(rows, c)
    msg_ref[rows : rows + 8, :] = pair_rows(one, two)
    fetched(0, source_refs, after_ref, sem)


def arrived(info, raw, sources):
    rows, cols, c = raw.shape
    return pl.pallas_call(
        functools.partial(arrive_kernel, len(sources)),
        out_shape=[result((cols, 2, rows // 2, c)), result((rows + 8, c)), result((3, 3, c, c))],
        in_specs=[SM, VM] + [HB] * len(sources),
        out_specs=[VM] * 3,
        scratch_shapes=[pltpu.SemaphoreType.DMA(())],
        compiler_params=room_for(raw, 4),
    )(info, raw, *far(sources))


def small_call(kernel, info, args, outs):
    total = sum(x.size for x in args) + sum(o.size for o in outs)
    return pl.pallas_call(
        kernel,
        out_shape=[result(o.shape) for o in outs],
        in_specs=[SM] * len(info) + [VM] * len(args),
        out_specs=[VM] * len(outs),
        compiler_params=pltpu.CompilerParams(vmem_limit_bytes=total * 8 + (2 << 20)),
    )(*info, *args)


def like(*shape):
    return jax.ShapeDtypeStruct(shape, F32)


def fold_kernel(by, info_ref, keep_ref, got_ref, out_ref, send_ref):
    n = out_ref.shape[0]
    upper = (info_ref[3] // by) % 2 == 1
    low = keep_ref[0:n, :] + got_ref[0:n, :]
    high = keep_ref[n:, :] + got_ref[n:, :]
    out_ref[...] = jnp.where(upper, high, low)
    send_ref[...] = jnp.where(upper, low, high)


def fold(info, by, keep, got):
    half = like(keep.shape[0] // 2, keep.shape[1])
    return small_call(functools.partial(fold_kernel, by), [info], [keep, got], [half, half])


def meet_kernel(info_ref, keep_ref, got_ref, out_ref, *square_refs):
    out = keep_ref[...] + got_ref[...]
    out_ref[...] = out
    for ref in square_refs:
        ref[...] = (out * out).reshape(-1, 8, out.shape[-1]).sum(0)


def meet(info, keep, got, squares=False):
    outs = [keep] + [like(8, keep.shape[1])] * squares
    return small_call(meet_kernel, [info], [keep, got], outs)


def unfold_kernel(by, info_ref, mine_ref, other_ref, out_ref):
    n = mine_ref.shape[0]
    upper = (info_ref[3] // by) % 2 == 1
    mine, other = mine_ref[...], other_ref[...]
    out_ref[0:n, :] = jnp.where(upper, other, mine)
    out_ref[n:, :] = jnp.where(upper, mine, other)


def unfold(info, by, mine, other):
    n, c = mine.shape
    return small_call(functools.partial(unfold_kernel, by), [info], [mine, other], [like(2 * n, c)])[0]


TABLE = 16


def spread_kernel(layers, rows, *refs):
    refs = list(refs)
    take = lambda n: [refs.pop(0) for _ in range(n)]
    infos = take(layers)
    parts_ref, square_ref, loss_ref = take(3)
    small = [0.0] * PAIR
    for l in range(layers):
        one_ref, bias1_ref, two_ref, bias2_ref = take(4)
        row = []
        for sums_ref, bias_ref in ((one_ref, bias1_ref), (two_ref, bias2_ref)):
            row += [sums_ref[rows + 1 : rows + 2, :], sums_ref[rows : rows + 1, :], bias_ref[0:1, :]]
        small[l % PAIR] += jnp.where(infos[l][2] == 1, jnp.concatenate(row, 0), 0.0)
    out_ref = take(1)[0]
    bands, n, c = parts_ref.shape
    share = parts_ref[...].sum(0)
    squares = square_ref[...].sum(0, keepdims=True) + (share * share).sum(0, keepdims=True)
    loss = loss_ref[rows : rows + 8, :].sum(0, keepdims=True)
    table = jnp.concatenate(small + [loss, squares, jnp.zeros((2, c), F32)], 0)
    for b in range(bands):
        out_ref[b, 0:n, :] = share
        out_ref[b, n : n + TABLE, :] = table


def spread(infos, rows, parts, square, loss, pieces):
    bands, n, c = parts.shape
    args = [parts, square, loss] + [x for piece in pieces for x in piece]
    kernel = functools.partial(spread_kernel, len(infos), rows)
    return small_call(kernel, infos, args, [like(bands, n + TABLE, c)])[0]


def table_kernel(info_ref, rest_ref, out_ref):
    out_ref[...] = rest_ref[:, rest_ref.shape[1] - TABLE :, :].sum(0)


def adam_step(w, first, second, grad, rate):
    first = 0.5 * first + 0.5 * grad
    second = 0.5 * second + 0.5 * grad * grad
    fix = 1.0 - 0.5**STEP
    step = first / fix / (jnp.sqrt(second / fix) + adam_eps) + decay_rate * w
    return w - rate * step, first, second


def tree_sum(items):
    while len(items) > 1:
        items = [a + b for a, b in zip(items[::2], items[1::2])]
    return items[0]


def adam_kernel(repeats, sections, *refs):
    refs = list(refs)
    take = lambda n: [refs.pop(0) for _ in range(n)]
    info_ref = take(1)[0]
    tables = [ref[...] for ref in take(sections)]
    rest_ref, got_rest_ref, odd_ref, got_odd_ref = take(4)
    small_refs = take(3)
    from_refs = take(3)
    new_small_refs = take(3)
    scalar_ref = take(1)[0]
    to_refs, old_refs, new_refs = take(3), take(3), take(3)
    in_sem, out_sem = refs
    bands = rest_ref.shape[0]
    n = from_refs[0].shape[1] // bands
    runs = [(which, run) for which in range(2) for run in range(bands)]

    def copies(sources, targets, sem, which, run):
        at = pl.ds(run * n, n)
        return [
            pltpu.make_async_copy(a.at[which, at], b.at[which, at], sem.at[k, which, run])
            for k, (a, b) in enumerate(zip(sources, targets))
        ]

    for which, run in runs:
        for copy in copies(from_refs, old_refs, in_sem, which, run):
            copy.start()
    chips = [tables[k] + tables[k + 1] for k in range(0, sections, PAIR)]
    squares = [jnp.sum(t[0:12] * t[0:12]) + jnp.sum(t[13:14]) for t in chips]
    norm = jnp.sqrt(jnp.full((8, 128), tree_sum(squares), F32))
    clip = clip_level / jnp.maximum(norm, clip_level)
    loss = jnp.full((8, 128), jnp.sum(chips[0][12:13]), F32) / repeats
    scalar_ref[0:8, :] = norm
    scalar_ref[8:16, :] = loss
    clip = clip[0:1, 0:1]
    first_core = info_ref[0] == 0
    grad = jnp.where(first_core, chips[0][0:6], chips[0][6:12]) * clip
    new = adam_step(*[ref[:, 0, :] for ref in small_refs], grad, rate_small)
    for ref, value in zip(new_small_refs, new):
        ref[:, 0, :] = value
    for which, run in runs:
        for copy in copies(from_refs, old_refs, in_sem, which, run):
            copy.wait()
        at = slice(run * n, (run + 1) * n)
        if which == 0:
            grad = jnp.where(first_core, rest_ref[run, 0:n, :], got_odd_ref[at, :])
        else:
            grad = jnp.where(first_core, got_rest_ref[run, 0:n, :], odd_ref[at, :])
        new = adam_step(*[ref[which, at, :] for ref in old_refs], grad * clip, rate_conv)
        for ref, value in zip(new_refs, new):
            ref[which, at, :] = value
        for copy in copies(new_refs, to_refs, out_sem, which, run):
            copy.start()
    for which, run in runs:
        for copy in copies(new_refs, to_refs, out_sem, which, run):
            copy.wait()


def optimizer(info, repeats, tables, rest, got_rest, odd, got_odd, smalls, states):
    shape, bands = states[0].shape, rest.shape[0]
    args = [*tables, rest, got_rest, odd, got_odd, *smalls]
    sems = pltpu.SemaphoreType.DMA((3, 2, bands))
    return pl.pallas_call(
        functools.partial(adam_kernel, repeats, len(tables)),
        out_shape=[like(*x.shape) for x in smalls] + [like(16, 128)] + [pltpu.HBM(shape, F32)] * 3,
        in_specs=[SM] + [VM] * len(args) + [HB] * 3,
        out_specs=[VM] * 4 + [HB] * 3,
        scratch_shapes=[pltpu.VMEM(shape, F32)] * 6 + [sems] * 2,
        compiler_params=pltpu.CompilerParams(vmem_limit_bytes=11 * states[0].size * 4),
    )(info, *args, *far(states))


def partner(x):
    return lax.ppermute(x, "section", [(i, i ^ 1) for i in range(lax.axis_size("section"))])


def to_image(bands, repeats):
    bands = jnp.repeat(bands, repeats, 0) if repeats > 1 else bands
    got = lax.all_to_all(bands, "band", 0, 0, tiled=True)
    return got.reshape(-1, *got.shape[2:])


def crossed(x, by):
    return lax.ppermute(x, "band", [(i, i ^ by) for i in range(lax.axis_size("band"))])


def band_bits():
    return [1 << k for k in range(lax.axis_size("band").bit_length() - 1)]


def swapped(parts):
    return lax.all_to_all(parts, "band", 0, 0, tiled=True)


def local(
    images,
    targets,
    masks,
    conv_weights,
    small_params,
    conv_first,
    conv_second,
    small_first,
    small_second,
):
    sections = lax.axis_size("section")
    bands = lax.axis_size("band")
    here = lax.axis_index("section")
    core = here % PAIR
    chip = here // PAIR
    chips = sections // PAIR
    layers = sections
    micro, part, width, c = images.shape
    repeats = bands // micro
    cols = width // PAIR
    rows = part * bands
    half = rows // 2

    image = to_image(lax.dynamic_slice_in_dim(images, core * cols, cols, 2), repeats)
    lengths = jnp.sum(masks.astype(F32), 2)
    counts = jnp.where(jnp.arange(part)[None, :] == 0, jnp.sum(lengths), 0.0)
    extra = jnp.stack([lengths, jnp.broadcast_to(counts, lengths.shape)] + [jnp.zeros_like(lengths)] * 6, 2)
    extra = jnp.broadcast_to(extra[..., None], (micro, part, 8, c))
    target = jnp.concatenate([lax.dynamic_slice_in_dim(targets, core * cols, cols, 2), extra], 2)
    image, target = lax.optimization_barrier((image, target))
    target = to_image(target, repeats)

    own = (conv_weights[0], jnp.pad(small_params[0], ((0, 2), (0, 0))))
    sources, smalls = [], []
    for k in range(chips):
        shift = [((i + PAIR * k) % sections, i) for i in range(sections)]
        theirs = own if k == 0 else tuple(lax.ppermute(x, "section", shift) for x in own)
        others = tuple(partner(x) for x in theirs)
        sources += [theirs[0], others[0]]
        smalls += [theirs[1], others[1]]
    smalls = jnp.stack(smalls)

    def pick_of(layer):
        return PAIR * ((layer // PAIR - chip) % chips) + (layer % PAIR != core).astype(jnp.int32)

    def info_of(layer):
        mine = (chip == layer // PAIR).astype(jnp.int32)
        active = (chip <= layer // PAIR).astype(jnp.int32)
        info = [core, pick_of(layer), mine, lax.axis_index("band"), active]
        return jnp.stack(info).astype(jnp.int32)

    def norms_of(layer):
        both = lax.dynamic_index_in_dim(smalls, pick_of(layer), 0, False)
        return jnp.pad(both[0:3], ((0, 5), (0, 0))), jnp.pad(both[3:6], ((0, 5), (0, 0)))

    infos = [info_of(l) for l in range(layers)]
    norms = [norms_of(l) for l in range(layers)]
    image, infos, norms = lax.optimization_barrier((image, infos, norms))
    again_first = not is_near(jax.ShapeDtypeStruct((cols, rows, c), F32))
    order = [(l, k) for l in range(layers) for k in range(2)]
    for l in reversed(range(layers)):
        order += [(l, 0)] * again_first + [(l, 1), (l, 0)]
    order = [(infos[l], k) for l, k in order[1:]] + [(infos[0], 0)]

    def with_next(w):
        return w, sources, order.pop(0)

    field, message, w = arrived(infos[0], image, sources)
    stack = []
    for l in range(layers):
        got = partner(message)
        mid, sent, norm, w = conv_forward(infos[l], with_next(w), field, got, message, norms[l][0])
        again = partner(sent)
        one, first_in = (field, got, norm), (field, got, message, norms[l][0])
        goal = (target, repeats) if l == layers - 1 else ()
        field, message, norm, w, *count = conv_forward(
            infos[l], with_next(w), mid, again, sent, norms[l][1], field, *goal
        )
        stack.append((one, (None if again_first else mid, again, norm), first_in))

    def second_back(l, w, t, got, enter, res):
        _, (v2, e2, n2), first_in = stack[l]
        if again_first:
            t, first_in = lax.optimization_barrier((t, first_in))
            v2, _, _, w = conv_forward(infos[l], with_next(w), *first_in)
        grad, grad_edge, t, sent, bias, w = conv_backward(
            infos[l], with_next(w), t, got, v2, n2, norms[l][1], norm=enter, res=res
        )
        return w, t, partner(sent), bias, (sent, v2, e2, n2, norms[l][1]), (grad, grad_edge)

    def grad_of(l, k, v, g, prev, other=None):
        _, edge, norm = stack[l][k]
        return kernel_grad(infos[l], v, edge, norm, norms[l][k], g, prev, other)

    grad, (count,) = field, count
    got = partner(message)
    loss_message = message

    t, enter, res = grad, None, None
    slots = [[None, None] for _ in range(PAIR)]
    pieces = {}
    for l in reversed(range(1, layers)):
        slot = slots[l % PAIR]
        w, t, got, bias2, enter, res = second_back(l, w, t, got, enter, res)
        k2 = grad_of(l, 1, enter[1], res[0], slot[1])
        sent = enter[0]
        v1, e1, n1 = stack[l][0]
        mid, _, t, message, bias1, w = conv_backward(
            infos[l], with_next(w), t, got, v1, n1, norms[l][0], norm=enter
        )
        got = partner(message)
        k1 = grad_of(l, 0, v1, mid, slot[0], k2 if l == 1 else None)
        enter = (message, v1, e1, n1, norms[l][0])
        slot[:] = [k1, k2]
        pieces[l] = (message, bias1, sent, bias2)

    keep, send = slots[1][0]
    info, bits = infos[0], band_bits()
    keep, send = fold(info, bits[0], keep, partner(send))
    got_odd = crossed(send, bits[0])
    w, t, got, bias2, enter, res = second_back(0, w, t, got, enter, res)
    mid, got_odd = lax.optimization_barrier((res[0], got_odd))
    keep, send = fold(info, bits[1], keep, got_odd)
    got_odd = crossed(send, bits[1])
    k2 = grad_of(0, 1, enter[1], mid, slots[0][1])
    t, k2, got_odd = lax.optimization_barrier((t, k2, got_odd))
    for by in bits[2:-1]:
        keep, send = fold(info, by, keep, got_odd)
        got_odd = crossed(send, by)
    keep, send = fold(info, bits[-1], keep, got_odd)
    mid, mid_edge, bias1 = norm_enter(t, got, enter)
    mid, send = lax.optimization_barrier((mid, send))
    got_odd = crossed(send, bits[-1])
    sent = enter[0]
    v1, e1, n1 = stack[0][0]
    even, send = grad_of(0, 0, v1, mid, slots[0][0], k2)
    even, send, got_odd = lax.optimization_barrier((even, send, got_odd))
    send = partner(send)
    odd, odd_square = meet(info, keep, got_odd, True)
    even, odd = lax.optimization_barrier((even, odd))
    odd_got = crossed(odd, bits[-1])
    _, _, _, message, _, _ = conv_backward(
        info, with_next(w), mid, mid_edge, v1, n1, norms[0][0]
    )
    pieces[0] = (message, bias1, sent, bias2)
    even, send, message, odd_got = lax.optimization_barrier((even, send, message, odd_got))
    even = meet(info, even, send)[0]
    odd = unfold(info, bits[-1], odd, odd_got)
    even, odd = lax.optimization_barrier((even, odd))
    odd_got = crossed(odd, bits[-2])
    parts = swapped(even.reshape(bands, -1, c))
    parts, odd_got = lax.optimization_barrier((parts, odd_got))
    odd = unfold(info, bits[-2], odd, odd_got)
    for by in bits[-3::-1]:
        odd = unfold(info, by, odd, crossed(odd, by))
    got_odd = partner(odd)
    rest = spread(infos, rows, parts, odd_square, loss_message, [pieces[l] for l in range(layers)])
    rest = swapped(rest)
    table = small_call(table_kernel, [info], [rest], [like(TABLE, c)])[0]
    got_rest = partner(rest)
    tables = [table]
    for by in range(1, sections):
        tables.append(lax.ppermute(table, "section", [(i, i ^ by) for i in range(sections)]))

    flat = lambda x: x.reshape(2, 9 * c, c)
    smalls = [x.transpose(1, 0, 2) for x in (small_params, small_first, small_second)]
    states = [flat(x) for x in (conv_weights, conv_first, conv_second)]
    *new_smalls, scalars, new_conv, new_conv_first, new_conv_second = optimizer(
        info, repeats, tables, rest, got_rest, odd, got_odd, smalls, states
    )
    new_conv, new_conv_first, new_conv_second = [
        x.reshape(conv_weights.shape) for x in (new_conv, new_conv_first, new_conv_second)
    ]
    new_small, new_small_first, new_small_second = [x.transpose(1, 0, 2) for x in new_smalls]
    grad_norm, loss_sum, valid_count = scalars[0, 0], scalars[8, 0], count[0, 0]
    return (
        new_conv,
        new_conv_first,
        new_conv_second,
        new_small,
        new_small_first,
        new_small_second,
        loss_sum,
        valid_count,
        grad_norm,
    )


def solution(mesh):
    in_specs = (
        P(None, "band", None, None),
        P(None, "band", None, None),
        P(None, "band", None),
        P("section", None, None, None, None, None),
        P("section", None, None),
        P("section", None, None, None, None, None),
        P("section", None, None, None, None, None),
        P("section", None, None),
        P("section", None, None),
    )
    out_specs = (
        P("section", None, None, None, None, None),
        P("section", None, None, None, None, None),
        P("section", None, None, None, None, None),
        P("section", None, None),
        P("section", None, None),
        P("section", None, None),
        P(),
        P(),
        P(),
    )
    return jax.shard_map(local, mesh=mesh, in_specs=in_specs, out_specs=out_specs, check_vma=False)
```
